128 devices in a mesh: wide: 64 (over y, x, z_hi, core), narrow: 2 (over z_lo).
Axes of the slice: x: 4, y: 4, z: 4 (z_hi: 2, z_lo: 2; z = z_hi * 2 + z_lo), core: 2. Of those that a mesh axis runs over, the one named last changes fastest.
Arguments:
- tokens: bfloat16 [16384, 1536], P('wide'), may hold values from -6 to 6
- doc_lengths: int32 [64, 4], P('wide'), may hold values from 1 to 128, 256 in all within a row
- norm_gain1: float32 [1536], replicated, may hold values from 0.5 to 1.5
- w_query: bfloat16 [1536, 1536], P('wide', 'narrow'), may hold values from -0.15625 to 0.15625
- b_query: float32 [1536], P('narrow'), may hold values from -3 to 3
- w_key: bfloat16 [1536, 256], P('wide', 'narrow'), may hold values from -0.15625 to 0.15625
- b_key: float32 [256], P('narrow'), may hold values from -3 to 3
- w_value: bfloat16 [1536, 256], P('wide', 'narrow'), may hold values from -0.15625 to 0.15625
- b_value: float32 [256], P('narrow'), may hold values from -3 to 3
- w_out: bfloat16 [1536, 1536], P('narrow', 'wide'), may hold values from -0.875 to 0.875
- norm_gain2: float32 [1536], replicated, may hold values from 0.5 to 1.5
- w_gate: bfloat16 [1536, 8960], P('wide', 'narrow'), may hold values from -0.15625 to 0.15625
- w_up: bfloat16 [1536, 8960], P('wide', 'narrow'), may hold values from -0.15625 to 0.15625
- w_down: bfloat16 [8960, 1536], P('narrow', 'wide'), may hold values from -0.0625 to 0.0625
- out_grad: bfloat16 [16384, 1536], P('wide'), may hold values from -16 to 16
Outputs:
- mixed_out: bfloat16 [16384, 1536], P('wide')
- grad_tokens: float32 [16384, 1536], P('wide')
- grad_gain1: float32 [1536], replicated
- grad_query: float32 [1536, 1536], P('wide', 'narrow')
- grad_qbias: float32 [1536], P('narrow')
- grad_key: float32 [1536, 256], P('wide', 'narrow')
- grad_kbias: float32 [256], P('narrow')
- grad_value: float32 [1536, 256], P('wide', 'narrow')
- grad_vbias: float32 [256], P('narrow')
- grad_outproj: float32 [1536, 1536], P('narrow', 'wide')
- grad_gain2: float32 [1536], replicated
- grad_gate: float32 [1536, 8960], P('wide', 'narrow')
- grad_up: float32 [1536, 8960], P('wide', 'narrow')
- grad_down: float32 [8960, 1536], P('narrow', 'wide')
The draws below stay inside these ranges and needn't reach their ends.
Inputs may be any that keep to these rules, and one draw needn't show every extreme that they name: `doc_lengths`: each pack's 4 document lengths are positive and sum to 256; the longest is exactly 128.
All inputs are finite; a program needn't handle non-finite values.
Results may differ from the reference program's by a relative error of at most 0.022.
Values may be sent and summed in bfloat16 or wider, within the bound.
No kernel may reach another device: no remote copies, remote signals or barrier semaphores. Data moves between devices by JAX's collectives and lax.ppermute only.
A program may use at most 256 MiB of HBM per device.

```python
import math
import jax
import jax.numpy as jnp
import numpy as np
from jax import lax

D = 1536
HEADS = 12
KV_HEADS = 2
HD = 128
FF = 8960
TOK_DEV = 256
DOCS = 4
GROUP = 6
PACKS = 64
TOKENS = 16384
N_WIDE = 64


def with_spikes(entries, own_key, source, target, parts, factor):
    owner, partner = [(jnp.arange(entries.shape[dim]) // (entries.shape[dim] // parts)).reshape([-1 if axis == dim else 1 for axis in range(entries.ndim)]) for dim in (source, target)]
    chosen = jax.random.permutation(own_key, parts)[partner]
    strong = (owner == chosen) | (owner == (partner + parts // 2) % parts)
    return jnp.where(strong, factor * entries, entries)


def levels(rng, dims, shards, low, largest):
    level, own = 1.0, jax.random.fold_in(rng, 6)
    for dim, parts in shards:
        draws = jnp.exp(jax.random.uniform(jax.random.fold_in(own, dim), (parts,), jnp.float32, low / len(shards), largest / len(shards)))
        level = level * jnp.repeat(draws, dims[dim] // parts).reshape([-1 if axis == dim else 1 for axis in range(len(dims))])
    return level


def profile(amount, total, most, lean):
    portions = [(1 << 20) // math.isqrt(standing ** lean) + 1 for standing in range(2, amount + 1)]
    rest, counts = total - most - (amount - 1), [1] * (amount - 1)
    while rest > 0:
        candidates = [i for i in range(amount - 1) if counts[i] < most]
        whole, budget = sum([portions[i] for i in candidates]), rest
        for i in candidates:
            more = min(most - counts[i], max(1, budget * portions[i] // whole), rest)
            counts[i] = counts[i] + more
            rest = rest - more
    return np.array([most] + counts)


def ragged(rng, count, total, reach, slope):
    if count == 2:
        one = jax.random.randint(rng, (), max(1, total - reach), min(reach, total - 1) + 1)
        return jnp.stack([one, total - one])
    sizes = jnp.asarray(profile(count, total, reach, slope), jnp.int32)
    twos = (count - 1) // 2
    giver, taker = sizes[1:1 + 2 * twos:2], sizes[2:2 + 2 * twos:2]
    slack = jnp.minimum(giver - 1, reach - taker)
    shifted = jax.random.randint(jax.random.fold_in(rng, 1), (twos,), 0, 1 << 20) % (slack + 1)
    sizes = sizes.at[1:1 + 2 * twos:2].set(giver - shifted).at[2:2 + 2 * twos:2].set(taker + shifted)
    return sizes[jax.random.permutation(jax.random.fold_in(rng, 2), count)]


def centred(key, shape, deviation, most, pieces=(), kind=jnp.bfloat16):
    gain = levels(key, shape, pieces, -0.22, 0.18) if pieces else 1.0
    entries = jax.random.normal(key, shape, jnp.float32) * deviation * gain
    return jnp.minimum(jnp.maximum(entries, -most), most).astype(kind)


def gaussian_with(own_key, extent, deviation, most, cuts, heavy, held_as=jnp.bfloat16):
    values = deviation * jax.random.normal(own_key, extent, jnp.float32)
    if cuts:
        values = values * levels(own_key, extent, cuts, -0.22, 0.18)
    return jnp.clip(with_spikes(values, jax.random.fold_in(own_key, 3), *heavy), -most, most).astype(held_as)


def setup_inputs(seed: int = 0) -> dict:
    seeds = jax.random.split(jax.random.key(seed), 16)
    tokens = centred(seeds[0], (TOKENS, D), 1.0, 6.0, ((0, 64),))
    doc_lengths = jax.vmap(lambda own: ragged(own, DOCS, TOK_DEV, TOK_DEV // 2, 1))(jax.random.split(seeds[1], PACKS)).reshape((PACKS, DOCS)).astype(jnp.int32)
    norm_gain1 = jnp.clip(1.0 + 0.1 * jax.random.normal(seeds[2], (D,), jnp.float32), 0.5, 1.5)
    w_query = centred(seeds[3], (D, HEADS * HD), D ** -0.5, 0.15625, ((0, 64), (1, 2)))
    b_query = centred(seeds[4], (HEADS * HD,), 0.5, 3.0, ((0, 2),), jnp.float32)
    w_key = centred(seeds[5], (D, KV_HEADS * HD), D ** -0.5, 0.15625, ((0, 64), (1, 2)))
    b_key = centred(seeds[6], (KV_HEADS * HD,), 0.5, 3.0, ((0, 2),), jnp.float32)
    w_value = centred(seeds[7], (D, KV_HEADS * HD), D ** -0.5, 0.15625, ((0, 64), (1, 2)))
    b_value = centred(seeds[8], (KV_HEADS * HD,), 0.5, 3.0, ((0, 2),), jnp.float32)
    w_out = centred(seeds[9], (HEADS * HD, D), (HEADS * HD // 32) ** -0.5, 0.875, ((0, 2), (1, 64)))
    norm_gain2 = jnp.clip(1.0 + 0.1 * jax.random.normal(seeds[10], (D,), jnp.float32), 0.5, 1.5)
    w_gate = centred(seeds[11], (D, FF), D ** -0.5, 0.15625, ((0, 64), (1, 2)))
    w_up = centred(seeds[12], (D, FF), D ** -0.5, 0.15625, ((0, 64), (1, 2)))
    w_down = centred(seeds[13], (FF, D), FF ** -0.5, 0.0625, ((0, 2), (1, 64)))
    out_grad = gaussian_with(seeds[14], (TOKENS, D), 1.0, 16.0, ((0, 64),), (0, 1, 64, 4.0))
    return dict(tokens=tokens, doc_lengths=doc_lengths, norm_gain1=norm_gain1, w_query=w_query, b_query=b_query, w_key=w_key, b_key=b_key, w_value=w_value, b_value=b_value, w_out=w_out, norm_gain2=norm_gain2, w_gate=w_gate, w_up=w_up, w_down=w_down, out_grad=out_grad)


@jax.custom_vjp
def low(v):
    return lax.optimization_barrier(v.astype(jnp.bfloat16)).astype(jnp.float32)

@jax.custom_vjp
def low_back(v):
    return v

def low_keep(v):
    return (low(v), None)

def low_pass(kept, grad):
    return (grad,)

def back_keep(v):
    return (v, None)

def back_low(kept, grad):
    return (low(grad),)
low.defvjp(low_keep, low_pass)
low_back.defvjp(back_keep, back_low)
rope_base = 10000.0
norm_eps = 1e-06

def mmul(left, right):
    return jnp.dot(left, right, precision=lax.Precision.HIGHEST)

def rms(value):
    return value * lax.rsqrt(lax.optimization_barrier(jnp.mean(value * value, axis=-1, keepdims=True)) + norm_eps)

def rotate(value, cosine, sine):
    half = value.shape[-1] // 2
    first = value[..., :half]
    second = value[..., half:]
    return jnp.concatenate([first * cosine - second * sine, second * cosine + first * sine], axis=-1)

def doc_layout(lengths):
    lengths = lengths.astype(jnp.int32)
    ends = jnp.cumsum(lengths).astype(jnp.int32)
    starts = (ends - lengths).astype(jnp.int32)
    place = jnp.arange(TOK_DEV, dtype=jnp.int32)
    segment = lax.optimization_barrier(jnp.sum((place[:, None] >= ends[None, :]).astype(jnp.int32), axis=1)).astype(jnp.int32)
    labels = jnp.arange(DOCS, dtype=jnp.int32)
    first = lax.optimization_barrier(jnp.sum(jnp.where(segment[:, None] == labels[None, :], starts[None, :], 0), axis=1)).astype(jnp.int32)
    return (segment, (place - first).astype(jnp.int32), place)

def pack_layer(inputs, lengths, weights):
    gain_one, w_query, b_query, w_key, b_key, w_value, b_value, w_out, gain_two, w_gate, w_up, w_down = weights
    segment, position, place = doc_layout(lengths)
    inverse = rope_base ** (-jnp.arange(0, HD, 2, dtype=jnp.float32) / HD)
    angle = position.astype(jnp.float32)[:, None] * inverse[None, :]
    cosine = jnp.cos(angle)[:, None, :]
    sine = jnp.sin(angle)[:, None, :]
    h_one = low(rms(inputs) * gain_one)
    q_lin = low_back(mmul(h_one, w_query) + b_query).reshape(TOK_DEV, HEADS, HD)
    k_lin = low_back(mmul(h_one, w_key) + b_key).reshape(TOK_DEV, KV_HEADS, HD)
    values = low(low_back(mmul(h_one, w_value) + b_value)).reshape(TOK_DEV, KV_HEADS, HD)
    queries = low(rotate(q_lin, cosine, sine)).reshape(TOK_DEV, KV_HEADS, GROUP, HD)
    keys = low(rotate(k_lin, cosine, sine))
    logits = jnp.einsum('ikgd,jkd->kgij', queries, keys, precision=lax.Precision.HIGHEST) * HD ** (-0.5)
    allowed = (segment[:, None] == segment[None, :]) & (place[None, :] <= place[:, None])
    logits = low_back(jnp.where(allowed[None, None], logits, -1000000000.0))
    top = lax.optimization_barrier(jnp.max(logits, axis=-1, keepdims=True))
    expo = jnp.exp(logits - top)
    probs = low(expo / lax.optimization_barrier(jnp.sum(expo, axis=-1, keepdims=True)))
    attended = jnp.einsum('kgij,jkd->ikgd', probs, values, precision=lax.Precision.HIGHEST)
    attended = low(low_back(attended.reshape(TOK_DEV, HEADS * HD)))
    resid = inputs + low_back(mmul(attended, w_out))
    h_two = low(rms(resid) * gain_two)
    gate = low_back(mmul(h_two, w_gate))
    up_act = low_back(mmul(h_two, w_up))
    hidden = low(gate * jax.nn.sigmoid(gate) * up_act)
    return resid + low_back(mmul(hidden, w_down))

def reference(tokens, doc_lengths, norm_gain1, w_query, b_query, w_key, b_key, w_value, b_value, w_out, norm_gain2, w_gate, w_up, w_down, out_grad):
    weights = tuple((item.astype(jnp.float32) for item in (norm_gain1, w_query, b_query, w_key, b_key, w_value, b_value, w_out, norm_gain2, w_gate, w_up, w_down)))
    packs = tokens.astype(jnp.float32).reshape(N_WIDE, TOK_DEV, D)

    def forward(pack_inputs, params):

        def single(item):
            return pack_layer(item[0], item[1], params)
        return lax.map(jax.checkpoint(single), (pack_inputs, doc_lengths))
    outputs, pullback = jax.vjp(forward, packs, weights)
    grad_packs, grads = pullback(out_grad.astype(jnp.float32).reshape(N_WIDE, TOK_DEV, D))
    mixed_out = outputs.reshape(TOKENS, D).astype(jnp.bfloat16)
    grad_tokens = grad_packs.reshape(TOKENS, D)
    return (mixed_out, grad_tokens, grads[0], grads[1], grads[2], grads[3], grads[4], grads[5], grads[6], grads[7], grads[8], grads[9], grads[10], grads[11])
```

```python
import jax
import jax.numpy as jnp
from jax import lax
from jax.sharding import Mesh, PartitionSpec as P

HD = 128
BF = jnp.bfloat16
F32 = jnp.float32
rope_base = 10000.0
norm_eps = 1e-06
WIDE = ("y", "x", "zh", "c")
EVERY = ("y", "x", "zh", "c", "zl")
SLICE = 1152


def mm(left, right):
    return jnp.dot(left, right, preferred_element_type=F32)


def contract_rows(left, right):
    return lax.dot_general(left, right, (((0,), (0,)), ((), ())), preferred_element_type=F32)


def contract_cols(left, right):
    return lax.dot_general(left, right, (((1,), (1,)), ((), ())), preferred_element_type=F32)


def hop(value, axis, step):
    size = lax.axis_size(axis)
    return lax.ppermute(value, axis, [(i, (i + step) % size) for i in range(size)])


def zhop(value, step):
    return lax.ppermute(value, ("zh", "zl"), [(i, (i + step) % 4) for i in range(4)])


def in_order(pieces, axis, me, dim):
    count = len(pieces)
    shape = list(pieces[0].shape)
    shape.insert(dim, count)
    whole = jnp.zeros(shape, pieces[0].dtype)
    for k, piece in enumerate(pieces):
        whole = lax.dynamic_update_index_in_dim(whole, piece, (me - k) % count, dim)
    return whole


def ring_pieces(value, axis):
    return [value, hop(value, axis, 1), hop(value, axis, 2), hop(value, axis, 3)]


def pair(mine, theirs, side, dim):
    first = jnp.where(side == 0, mine, theirs)
    second = jnp.where(side == 0, theirs, mine)
    return jnp.stack([first, second], dim)


def gather_rows(value, spot):
    y, x, zh, c = spot
    cols = value.shape[1]
    both = pair(value, hop(value, "zh", 1), zh, 0)
    half = cols // 2
    left, right = both[..., :half], both[..., half:]
    left = in_order(ring_pieces(left, "x"), "x", x, 0)
    right = in_order(ring_pieces(right, "y"), "y", y, 0)
    left = in_order(ring_pieces(left, "y"), "y", y, 0)
    right = in_order(ring_pieces(right, "x"), "x", x, 1)
    whole = jnp.concatenate([left, right], -1)
    other = hop(whole, "c", 1)
    return pair(whole, other, c, 3).reshape(1536, cols)


def trade(blocks, zh, c):
    me = zh * 2 + c
    got = []
    for k in range(4):
        block = lax.dynamic_index_in_dim(blocks, me ^ k, 0, keepdims=False)
        if k:
            block = lax.ppermute(block, ("zh", "c"), [(i, i ^ k) for i in range(4)])
        got.append(block)
    whole = jnp.zeros(blocks.shape, blocks.dtype)
    for k in range(4):
        whole = lax.dynamic_update_index_in_dim(whole, got[k], me ^ k, 0)
    return whole


def gather_tokens(value):
    ring = jnp.concatenate([value, zhop(value, 1), zhop(value, 3), zhop(value, 2)], 0)
    return jnp.concatenate([ring, hop(ring, "c", 1)], 0)


def sum_tokens(part):
    half = part.shape[0] // 2
    quarter = half // 4
    mine = part[:half].astype(F32) + hop(part[half:].astype(BF), "c", 1).astype(F32)
    sent = mine.astype(BF)
    back = zhop(sent[quarter : 2 * quarter], 3)
    ahead = zhop(sent[2 * quarter : 3 * quarter], 1)
    far = zhop(sent[3 * quarter :], 2)
    return mine[:quarter] + back.astype(F32) + ahead.astype(F32) + far.astype(F32)


def rotate(value, cosine, sine):
    half = value.shape[-1] // 2
    first = value[..., :half]
    second = value[..., half:]
    return jnp.concatenate(
        [first * cosine - second * sine, second * cosine + first * sine], axis=-1
    )


def doc_layout(lengths, count):
    ends = jnp.cumsum(lengths)
    starts = ends - lengths
    place = jnp.arange(count, dtype=jnp.int32)
    segment = jnp.sum((place[:, None] >= ends[None, :]).astype(jnp.int32), axis=1)
    labels = jnp.arange(lengths.shape[0], dtype=jnp.int32)
    first = jnp.sum(jnp.where(segment[:, None] == labels[None, :], starts[None, :], 0), axis=1)
    return (segment, place - first, place)


def own_rows(value, side):
    half = value.shape[0] // 2
    return lax.dynamic_slice_in_dim(value, side * half, half, 0)


def both_rows(mine, zl):
    return pair(mine, hop(mine, "zl", 1), zl, 0).reshape(2 * mine.shape[0], mine.shape[1])


def on_device(
    tokens,
    doc_lengths,
    norm_gain1,
    w_query,
    b_query,
    w_key,
    b_key,
    w_value,
    b_value,
    w_out,
    norm_gain2,
    w_gate,
    w_up,
    w_down,
    out_grad,
):
    y, x, zh, c, zl = (lax.axis_index(axis) for axis in EVERY)
    spot = (y, x, zh, c)
    rows = tokens.shape[0]
    hidden_units = w_gate.shape[1]
    pad = 4 * SLICE - hidden_units
    scale = HD ** (-0.5)

    qkv_full = gather_rows(jnp.concatenate([w_query, w_key, w_value], 1), spot)
    out_full = gather_rows(w_out.T, spot)
    ffn = jnp.stack([w_gate, w_up, w_down.T], 1)
    ffn = jnp.pad(ffn, ((0, 0), (0, 0), (0, pad))).reshape(24, 3, 4, SLICE)
    ffn = trade(ffn.transpose(2, 0, 1, 3).reshape(4, 24, 3 * SLICE), zh, c)
    ffn_full = lax.all_gather(ffn.reshape(96, 3 * SLICE), ("y", "x"), axis=0, tiled=True)
    gate_up_full, down_full = ffn_full[:, : 2 * SLICE], ffn_full[:, 2 * SLICE :]
    grad_all = gather_tokens(own_rows(out_grad, zl))

    local_heads = w_query.shape[1] // HD
    segment, position, place = doc_layout(doc_lengths[0], rows)
    inverse = rope_base ** (-jnp.arange(0, HD, 2, dtype=F32) / HD)
    angle = position.astype(F32)[:, None] * inverse[None, :]
    cosine = jnp.cos(angle)[:, None, :]
    sine = jnp.sin(angle)[:, None, :]
    allowed = (segment[:, None] == segment[None, :]) & (place[None, :] <= place[:, None])
    inputs = tokens.astype(F32)
    factor_one = lax.rsqrt(jnp.mean(inputs * inputs, axis=-1, keepdims=True) + norm_eps)
    normed_one = inputs * factor_one
    h_one = (normed_one * norm_gain1).astype(BF)
    qkv = mm(h_one, qkv_full) + jnp.concatenate([b_query, b_key, b_value])
    q_cols = local_heads * HD
    queries = rotate(qkv[:, :q_cols].reshape(rows, local_heads, HD), cosine, sine).astype(BF)
    keys = rotate(qkv[:, q_cols : q_cols + HD].reshape(rows, 1, HD), cosine, sine)
    keys = keys.astype(BF).reshape(rows, HD)
    values = qkv[:, q_cols + HD :].astype(BF)
    logits = jnp.einsum("igd,jd->gij", queries, keys, preferred_element_type=F32) * scale
    logits = jnp.where(allowed[None], logits, -1000000000.0)
    top = jnp.max(logits, axis=-1, keepdims=True)
    expo = jnp.exp(logits - top)
    probs = expo / jnp.sum(expo, axis=-1, keepdims=True)
    probs_low = probs.astype(BF)
    attended = jnp.einsum("gij,jd->igd", probs_low, values, preferred_element_type=F32)
    attended = attended.reshape(rows, q_cols).astype(BF)
    branch = contract_cols(attended, out_full)
    theirs = hop(own_rows(branch, 1 - zl).astype(BF), "zl", 1)
    resid = own_rows(tokens, zl).astype(F32) + own_rows(branch, zl) + theirs.astype(F32)

    factor_two = lax.rsqrt(jnp.mean(resid * resid, axis=-1, keepdims=True) + norm_eps)
    normed_two = resid * factor_two
    h_two = gather_tokens((normed_two * norm_gain2).astype(BF))
    gate_up = mm(h_two, gate_up_full)
    grad_hidden = mm(grad_all, down_full)
    gate, up_act = gate_up[:, :SLICE], gate_up[:, SLICE:]
    sigma = jax.nn.sigmoid(gate)
    swish = gate * sigma
    hidden = (swish * up_act).astype(BF)
    grad_gate_act = (grad_hidden * up_act * sigma * (1.0 + gate * (1.0 - sigma))).astype(BF)
    grad_up_act = (grad_hidden * swish).astype(BF)
    grad_act = jnp.concatenate([grad_gate_act, grad_up_act], 1)
    grad_h_two = sum_tokens(contract_cols(grad_act, gate_up_full))
    d_ffn = jnp.concatenate(
        [contract_rows(h_two, grad_act).astype(BF), contract_rows(grad_all, hidden).astype(BF)], 1
    )
    mixed = (resid + sum_tokens(contract_cols(hidden, down_full))).astype(BF)
    mixed_out = both_rows(mixed, zl)
    d_ffn = lax.psum_scatter(d_ffn, ("y", "x"), scatter_dimension=0, tiled=True)
    d_ffn = trade(d_ffn.reshape(4, 24, 3 * SLICE), zh, c).astype(F32)
    d_ffn = d_ffn.reshape(4, 24, 3, SLICE).transpose(2, 1, 0, 3).reshape(3, 24, 4 * SLICE)
    d_gate, d_up, d_down = (d_ffn[i, :, :hidden_units] for i in range(3))

    gain_two_term = jnp.sum(grad_h_two * normed_two, axis=0)
    grad_n_two = grad_h_two * norm_gain2
    grad_resid = own_rows(out_grad, zl).astype(F32) + factor_two * (
        grad_n_two - normed_two * jnp.mean(grad_n_two * normed_two, axis=-1, keepdims=True)
    )
    grad_branch = both_rows(grad_resid.astype(BF), zl)
    d_out = contract_rows(grad_branch, attended)
    grad_att = mm(grad_branch, out_full).astype(BF).reshape(rows, local_heads, HD)

    grad_probs = jnp.einsum("igd,jd->gij", grad_att, values, preferred_element_type=F32)
    grad_vraw = jnp.einsum("gij,igd->jd", probs_low, grad_att, preferred_element_type=F32)
    inner = jnp.sum(probs * grad_probs, axis=-1, keepdims=True)
    grad_logits = (probs * (grad_probs - inner)).astype(BF)
    grad_qrot = jnp.einsum("gij,jd->igd", grad_logits, keys, preferred_element_type=F32) * scale
    grad_krot = jnp.einsum("gij,igd->jd", grad_logits, queries, preferred_element_type=F32) * scale
    grad_qlin = rotate(grad_qrot, cosine, -sine).reshape(rows, q_cols).astype(BF)
    grad_klin = rotate(grad_krot[:, None, :], cosine, -sine).reshape(rows, HD).astype(BF)
    grad_qkv = jnp.concatenate([grad_qlin, grad_klin, grad_vraw.astype(BF)], 1)
    d_qkv = contract_rows(h_one, grad_qkv)
    bias_term = jnp.sum(grad_qkv.astype(F32), axis=0)

    grad_h_part = contract_cols(grad_qkv, qkv_full)
    theirs = hop(own_rows(grad_h_part, 1 - zl).astype(BF), "zl", 1)
    grad_h_one = own_rows(grad_h_part, zl) + theirs.astype(F32)
    my_normed = own_rows(normed_one, zl)
    gain_one_term = jnp.sum(grad_h_one * my_normed, axis=0)
    grad_n_one = grad_h_one * norm_gain1
    grad_tokens = grad_resid + own_rows(factor_one, zl) * (
        grad_n_one - my_normed * jnp.mean(grad_n_one * my_normed, axis=-1, keepdims=True)
    )
    grad_tokens = both_rows(grad_tokens.astype(BF), zl).astype(F32)

    d_attn = jnp.concatenate([d_qkv.astype(BF), d_out.astype(BF)], 1)
    d_attn = sum_rows(d_attn, spot)
    cols = qkv_full.shape[1]
    d_query, d_key, d_value, d_outproj = jnp.split(d_attn, [q_cols, q_cols + HD, cols], 1)
    gain_one, gain_two = lax.psum((gain_one_term, gain_two_term), EVERY)
    bias = lax.psum(bias_term, WIDE)
    d_qbias, d_kbias, d_vbias = jnp.split(bias, [q_cols, q_cols + HD])
    return (
        mixed_out,
        grad_tokens,
        gain_one,
        d_query,
        d_qbias,
        d_key,
        d_kbias,
        d_value,
        d_vbias,
        d_outproj.T,
        gain_two,
        d_gate,
        d_up,
        d_down.T,
    )


def ring_sum(value, axis, me, dim):
    def block(k):
        return lax.dynamic_index_in_dim(value, (me + k) % 4, dim, keepdims=False)

    total = block(0).astype(F32)
    for k in (1, 2, 3):
        total = total + hop(block(k), axis, k).astype(F32)
    return total


def sum_rows(value, spot):
    y, x, zh, c = spot
    cols = value.shape[1]
    value = value.reshape(4, 4, 2, 2, 24, cols)
    mine = lax.dynamic_index_in_dim(value, c, 3, keepdims=False)
    other = lax.dynamic_index_in_dim(value, 1 - c, 3, keepdims=False)
    value = (mine.astype(F32) + hop(other, "c", 1).astype(F32)).astype(BF)
    half = cols // 2
    left, right = value[..., :half], value[..., half:]
    left = ring_sum(left, "y", y, 0).astype(BF)
    right = ring_sum(right, "x", x, 1).astype(BF)
    left = ring_sum(left, "x", x, 0)
    right = ring_sum(right, "y", y, 0)
    both = jnp.concatenate([left, right], -1)
    mine = lax.dynamic_index_in_dim(both, zh, 0, keepdims=False)
    other = lax.dynamic_index_in_dim(both, 1 - zh, 0, keepdims=False)
    return mine + hop(other.astype(BF), "zh", 1).astype(F32)


def solution(mesh):
    split = Mesh(mesh.devices.reshape(4, 4, 2, 2, 2), EVERY)
    return jax.shard_map(
        on_device,
        mesh=split,
        in_specs=(
            P(WIDE, None),
            P(WIDE, None),
            P(),
            P(WIDE, "zl"),
            P("zl"),
            P(WIDE, "zl"),
            P("zl"),
            P(WIDE, "zl"),
            P("zl"),
            P("zl", WIDE),
            P(),
            P(WIDE, "zl"),
            P(WIDE, "zl"),
            P("zl", WIDE),
            P(WIDE, None),
        ),
        out_specs=(
            P(WIDE, None),
            P(WIDE, None),
            P(),
            P(WIDE, "zl"),
            P("zl"),
            P(WIDE, "zl"),
            P("zl"),
            P(WIDE, "zl"),
            P("zl"),
            P("zl", WIDE),
            P(),
            P(WIDE, "zl"),
            P(WIDE, "zl"),
            P("zl", WIDE),
        ),
        check_vma=False,
    )
```

```python
import jax
import jax.numpy as jnp
from jax import lax
from jax.experimental import pallas as pl
from jax.experimental.pallas import tpu as pltpu
from jax.sharding import Mesh, PartitionSpec as P

HD = 128
BF = jnp.bfloat16
F32 = jnp.float32
rope_base = 10000.0
norm_eps = 1e-06
WIDE = ("y", "x", "zh", "c")
EVERY = ("y", "x", "zh", "c", "zl")
SLICE = 1152
ATT = 896
LEFT = 512
HEADS = 6


def mm(left, right):
    return jnp.dot(left, right, preferred_element_type=F32)


def contract_rows(left, right):
    return lax.dot_general(left, right, (((0,), (0,)), ((), ())), preferred_element_type=F32)


def contract_cols(left, right):
    return lax.dot_general(left, right, (((1,), (1,)), ((), ())), preferred_element_type=F32)


def hop(value, axis, step):
    size = lax.axis_size(axis)
    return lax.ppermute(value, axis, [(i, (i + step) % size) for i in range(size)])


def zhop(value, step):
    return lax.ppermute(value, ("zh", "zl"), [(i, (i + step) % 4) for i in range(4)])


def put(whole, piece, spots):
    return lax.dynamic_update_slice(whole, piece, spots)


def ring_pieces(value, axis):
    return [(0, value)] + [(k, hop(value, axis, k)) for k in (1, 3, 2)]


def pair(mine, theirs, side, dim):
    first = jnp.where(side == 0, mine, theirs)
    second = jnp.where(side == 0, theirs, mine)
    return jnp.stack([first, second], dim)


def quad_hop(value, flip):
    return lax.ppermute(value, ("zh", "c"), [(i, i ^ flip) for i in range(4)])


def gather_attn(value, spot):
    y, x, zh, c = spot
    me = zh * 2 + c
    mine = lax.dynamic_index_in_dim(value, c, 0)
    other = lax.dynamic_index_in_dim(value, 1 - c, 0)
    block = jnp.zeros((4, 24, ATT), value.dtype)
    block = put(block, mine, (me, 0, 0))
    for flip, sent in ((1, other), (2, mine), (3, other)):
        block = put(block, quad_hop(sent, flip), (me ^ flip, 0, 0))
    block = block.reshape(1, 96, ATT)
    left = jnp.zeros((4, 96, LEFT), value.dtype)
    for k, piece in ring_pieces(block[..., :LEFT], "x"):
        left = put(left, piece, ((x - k) % 4, 0, 0))
    right = jnp.zeros((4, 96, ATT - LEFT), value.dtype)
    for k, piece in ring_pieces(block[..., LEFT:], "y"):
        right = put(right, piece, ((y - k) % 4, 0, 0))
    half = jnp.zeros((4, 4, 96, ATT), value.dtype)
    for k, piece in ring_pieces(left[None], "y"):
        half = put(half, piece, ((y - k) % 4, 0, 0, 0))
    for k, piece in ring_pieces(right[:, None], "x"):
        half = put(half, piece, (0, (x - k) % 4, 0, LEFT))
    half = half.reshape(1, 1536, ATT)
    whole = jnp.zeros((2, 1536, ATT), value.dtype)
    whole = put(whole, half, (c, 0, 0))
    return put(whole, hop(half, "c", 1), (1 - c, 0, 0))


def ring_sum(value, axis, me, dim):
    def block(k):
        return lax.dynamic_index_in_dim(value, (me + k) % 4, dim, keepdims=False)

    total = block(0).astype(F32)
    for k in (1, 3, 2):
        total = total + hop(block(k), axis, k).astype(F32)
    return total


def scatter_attn(value, spot):
    y, x, zh, c = spot
    me = zh * 2 + c
    mine = lax.dynamic_index_in_dim(value, c, 0, keepdims=False)
    other = lax.dynamic_index_in_dim(value, 1 - c, 0, keepdims=False)
    part = (mine.astype(F32) + hop(other, "c", 1).astype(F32)).astype(BF)
    part = part.reshape(4, 4, 96, ATT)
    left = ring_sum(part[..., :LEFT], "y", y, 0).astype(BF)
    right = ring_sum(part[..., LEFT:], "x", x, 1).astype(BF)
    left = ring_sum(left, "x", x, 0)
    right = ring_sum(right, "y", y, 0)
    part = jnp.concatenate([left, right], -1).reshape(4, 24, ATT)

    def block(flip):
        return lax.dynamic_index_in_dim(part, me ^ flip, 0, keepdims=False)

    got = [quad_hop(block(flip).astype(BF), flip).astype(F32) for flip in (1, 2, 3)]
    return pair(block(0) + got[1], got[0] + got[2], c, 0)


def sum_vectors(value, spot):
    y, x, zh, c = spot
    zl = lax.axis_index("zl")
    value = value + hop(value, "c", 1)
    for axis, me in (("x", x), ("y", y)):
        whole = jnp.zeros((4,) + value.shape, F32)
        for k, piece in ring_pieces(value, axis):
            whole = put(whole, piece[None], ((me - k) % 4, 0, 0))
        value = (whole[0] + whole[1]) + (whole[2] + whole[3])
    value = value + hop(value, "zh", 1)
    return jnp.concatenate([value[:24] + hop(value[:24], "zl", 1), value[24:]], 0)


def trade(blocks, zh, c):
    me = zh * 2 + c
    got = []
    for k in range(4):
        block = lax.dynamic_index_in_dim(blocks, me ^ k, 0, keepdims=False)
        if k:
            block = lax.ppermute(block, ("zh", "c"), [(i, i ^ k) for i in range(4)])
        got.append(block)
    whole = jnp.zeros(blocks.shape, blocks.dtype)
    for k in range(4):
        whole = lax.dynamic_update_index_in_dim(whole, got[k], me ^ k, 0)
    return whole


def gather_tokens(value):
    ring = jnp.concatenate([value, zhop(value, 1), zhop(value, 3), zhop(value, 2)], 0)
    return jnp.concatenate([ring, hop(ring, "c", 1)], 0)


def sum_tokens(part):
    half = part.shape[0] // 2
    quarter = half // 4
    mine = part[:half].astype(F32) + hop(part[half:].astype(BF), "c", 1).astype(F32)
    sent = mine.astype(BF)
    back = zhop(sent[quarter : 2 * quarter], 3)
    ahead = zhop(sent[2 * quarter : 3 * quarter], 1)
    far = zhop(sent[3 * quarter :], 2)
    return mine[:quarter] + back.astype(F32) + ahead.astype(F32) + far.astype(F32)


def halves(side, value, mine_ref, theirs_ref):
    half = value.shape[0] // 2
    low, high = value[:half], value[half:]
    first = side == 0
    mine_ref[...] = jnp.where(first, low, high)
    theirs_ref[...] = jnp.where(first, high, low).astype(BF)


def turn(value, cosine, sine):
    return value * cosine + pltpu.roll(value, HD // 2, 1) * sine


def attention_kernel(
    side, h, w, bias, cosine, sine, keep, mine, theirs, attended, qkv_out, probs_out
):
    scale = HD ** (-0.5)
    cos, sin = cosine[...], sine[...]
    allowed = keep[...] > 0.5
    q_cols = HEADS * HD
    first = mm(h[...], w[0]) + bias[:, :ATT]
    keys = turn(first[:, q_cols:], cos, sin).astype(BF)
    values = (mm(h[...], w[1, :, :HD]) + bias[:, ATT:]).astype(BF)
    qkv_out[:, q_cols : q_cols + HD] = keys
    qkv_out[:, q_cols + HD :] = values
    for g in range(HEADS):
        cols = slice(g * HD, (g + 1) * HD)
        query = turn(first[:, cols], cos, sin).astype(BF)
        qkv_out[:, cols] = query
        logits = jnp.where(allowed, contract_cols(query, keys) * scale, -1000000000.0)
        expo = jnp.exp(logits - jnp.max(logits, axis=-1, keepdims=True))
        probs = expo / jnp.sum(expo, axis=-1, keepdims=True)
        probs_out[g] = probs
        attended[:, cols] = mm(probs.astype(BF), values).astype(BF)
    halves(side[0], contract_cols(attended[...], w[1, :, HD:]), mine, theirs)


def attention_forward(side, h, w, bias, cosine, sine, keep):
    rows, d = h.shape
    return pl.pallas_call(
        attention_kernel,
        in_specs=[pl.BlockSpec(memory_space=pltpu.SMEM)]
        + [pl.BlockSpec(memory_space=pltpu.VMEM)] * 6,
        out_shape=(
            jax.ShapeDtypeStruct((rows // 2, d), F32),
            jax.ShapeDtypeStruct((rows // 2, d), BF),
            jax.ShapeDtypeStruct((rows, HEADS * HD), BF),
            jax.ShapeDtypeStruct((rows, (HEADS + 2) * HD), BF),
            jax.ShapeDtypeStruct((HEADS, rows, rows), F32),
        ),
        compiler_params=pltpu.CompilerParams(vmem_limit_bytes=48 * 2**20),
        cost_estimate=pl.CostEstimate(
            flops=2_200_000_000, bytes_accessed=12_000_000, transcendentals=400_000
        ),
    )(side, h, w, bias, cosine, sine, keep)


def attention_back_kernel(
    side, branch, h, w, attended, qkv, probs, cosine, sine, mine, theirs, grads, bias, grad_qkv
):
    scale = HD ** (-0.5)
    cos, sin = cosine[...], -sine[...]
    q_cols = HEADS * HD
    keys = qkv[:, q_cols : q_cols + HD]
    values = qkv[:, q_cols + HD :]
    grad_att = mm(branch[...], w[1, :, HD:]).astype(BF)
    grad_key = jnp.zeros((branch.shape[0], HD), F32)
    grad_value = jnp.zeros((branch.shape[0], HD), F32)
    for g in range(HEADS):
        cols = slice(g * HD, (g + 1) * HD)
        grad_head = grad_att[:, cols]
        grad_probs = contract_cols(grad_head, values)
        prob = probs[g]
        inner = jnp.sum(prob * grad_probs, axis=-1, keepdims=True)
        grad_logits = (prob * (grad_probs - inner)).astype(BF)
        grad_query = mm(grad_logits, keys) * scale
        grad_qkv[:, cols] = turn(grad_query, cos, sin).astype(BF)
        grad_key += contract_rows(grad_logits, qkv[:, cols])
        grad_value += contract_rows(prob.astype(BF), grad_head)
    grad_qkv[:, q_cols : q_cols + HD] = turn(grad_key * scale, cos, sin).astype(BF)
    grad_qkv[:, q_cols + HD :] = grad_value.astype(BF)
    bias[...] = jnp.sum(grad_qkv[...].astype(F32), axis=0, keepdims=True)
    grads[0] = contract_rows(h[...], grad_qkv[:, :ATT]).astype(BF)
    grads[1, :, :HD] = contract_rows(h[...], grad_qkv[:, ATT:]).astype(BF)
    grads[1, :, HD:] = contract_rows(branch[...], attended[...]).astype(BF)
    grad_h = contract_cols(grad_qkv[:, :ATT], w[0])
    grad_h += contract_cols(grad_qkv[:, ATT:], w[1, :, :HD])
    halves(side[0], grad_h, mine, theirs)


def attention_backward(side, branch, h, w, attended, qkv, probs, cosine, sine):
    rows, d = h.shape
    return pl.pallas_call(
        attention_back_kernel,
        in_specs=[pl.BlockSpec(memory_space=pltpu.SMEM)]
        + [pl.BlockSpec(memory_space=pltpu.VMEM)] * 8,
        out_shape=(
            jax.ShapeDtypeStruct((rows // 2, d), F32),
            jax.ShapeDtypeStruct((rows // 2, d), BF),
            jax.ShapeDtypeStruct(w.shape, BF),
            jax.ShapeDtypeStruct((1, (HEADS + 2) * HD), F32),
        ),
        scratch_shapes=[pltpu.VMEM((rows, (HEADS + 2) * HD), BF)],
        compiler_params=pltpu.CompilerParams(vmem_limit_bytes=48 * 2**20),
        cost_estimate=pl.CostEstimate(
            flops=4_300_000_000, bytes_accessed=20_000_000, transcendentals=0
        ),
    )(side, branch, h, w, attended, qkv, probs, cosine, sine)


def doc_layout(lengths, count):
    ends = jnp.cumsum(lengths)
    starts = ends - lengths
    place = jnp.arange(count, dtype=jnp.int32)
    segment = jnp.sum((place[:, None] >= ends[None, :]).astype(jnp.int32), axis=1)
    labels = jnp.arange(lengths.shape[0], dtype=jnp.int32)
    first = jnp.sum(jnp.where(segment[:, None] == labels[None, :], starts[None, :], 0), axis=1)
    return (segment, place - first, place)


def own_rows(value, side):
    half = value.shape[0] // 2
    return lax.dynamic_slice_in_dim(value, side * half, half, 0)


def both_rows(mine, zl):
    return pair(mine, hop(mine, "zl", 1), zl, 0).reshape(2 * mine.shape[0], mine.shape[1])


def on_device(
    tokens,
    doc_lengths,
    norm_gain1,
    w_query,
    b_query,
    w_key,
    b_key,
    w_value,
    b_value,
    w_out,
    norm_gain2,
    w_gate,
    w_up,
    w_down,
    out_grad,
):
    y, x, zh, c, zl = (lax.axis_index(axis) for axis in EVERY)
    spot = (y, x, zh, c)
    rows = tokens.shape[0]
    hidden_units = w_gate.shape[1]
    pad = 4 * SLICE - hidden_units

    side = zl.reshape(1)
    attn = jnp.concatenate([w_query, w_key, w_value, w_out.T], 1)
    attn = jnp.stack([attn[:, :ATT], attn[:, ATT:]], 0)
    attn_full = gather_attn(attn, spot)
    ffn = jnp.stack([w_gate, w_up, w_down.T], 1)
    ffn = jnp.pad(ffn, ((0, 0), (0, 0), (0, pad))).reshape(24, 3, 4, SLICE)
    ffn = trade(ffn.transpose(2, 0, 1, 3).reshape(4, 24, 3 * SLICE), zh, c)
    ffn_full = lax.all_gather(ffn.reshape(96, 3 * SLICE), ("y", "x"), axis=0, tiled=True)
    gate_up_full, down_full = ffn_full[:, : 2 * SLICE], ffn_full[:, 2 * SLICE :]
    grad_all = gather_tokens(own_rows(out_grad, zl))

    segment, position, place = doc_layout(doc_lengths[0], rows)
    inverse = rope_base ** (-jnp.arange(0, HD, 2, dtype=F32) / HD)
    angle = position.astype(F32)[:, None] * inverse[None, :]
    cosine, sine = jnp.cos(angle), jnp.sin(angle)
    cosine = jnp.concatenate([cosine, cosine], 1)
    sine = jnp.concatenate([-sine, sine], 1)
    keep = (segment[:, None] == segment[None, :]) & (place[None, :] <= place[:, None])
    inputs = tokens.astype(F32)
    factor_one = lax.rsqrt(jnp.mean(inputs * inputs, axis=-1, keepdims=True) + norm_eps)
    normed_one = inputs * factor_one
    h_one = (normed_one * norm_gain1).astype(BF)
    bias = jnp.concatenate([b_query, b_key, b_value])[None]
    mine, theirs, attended, qkv, probs = attention_forward(
        side, h_one, attn_full, bias, cosine, sine, keep.astype(F32)
    )
    theirs = hop(theirs, "zl", 1)
    resid = own_rows(tokens, zl).astype(F32) + mine + theirs.astype(F32)

    factor_two = lax.rsqrt(jnp.mean(resid * resid, axis=-1, keepdims=True) + norm_eps)
    normed_two = resid * factor_two
    h_two = gather_tokens((normed_two * norm_gain2).astype(BF))
    gate_up = mm(h_two, gate_up_full)
    grad_hidden = mm(grad_all, down_full)
    gate, up_act = gate_up[:, :SLICE], gate_up[:, SLICE:]
    sigma = jax.nn.sigmoid(gate)
    swish = gate * sigma
    hidden = (swish * up_act).astype(BF)
    grad_gate_act = (grad_hidden * up_act * sigma * (1.0 + gate * (1.0 - sigma))).astype(BF)
    grad_up_act = (grad_hidden * swish).astype(BF)
    grad_act = jnp.concatenate([grad_gate_act, grad_up_act], 1)
    grad_h_two = sum_tokens(contract_cols(grad_act, gate_up_full))
    d_ffn = jnp.concatenate(
        [contract_rows(h_two, grad_act).astype(BF), contract_rows(grad_all, hidden).astype(BF)], 1
    )
    mixed = (resid + sum_tokens(contract_cols(hidden, down_full))).astype(BF)
    mixed_out = both_rows(mixed, zl)
    d_ffn = lax.psum_scatter(d_ffn, ("y", "x"), scatter_dimension=0, tiled=True)
    d_ffn = trade(d_ffn.reshape(4, 24, 3 * SLICE), zh, c).astype(F32)
    d_ffn = d_ffn.reshape(4, 24, 3, SLICE).transpose(2, 1, 0, 3).reshape(3, 24, 4 * SLICE)
    d_gate, d_up, d_down = (d_ffn[i, :, :hidden_units] for i in range(3))

    gain_two_term = jnp.sum(grad_h_two * normed_two, axis=0)
    grad_n_two = grad_h_two * norm_gain2
    grad_resid = own_rows(out_grad, zl).astype(F32) + factor_two * (
        grad_n_two - normed_two * jnp.mean(grad_n_two * normed_two, axis=-1, keepdims=True)
    )
    grad_branch = both_rows(grad_resid.astype(BF), zl)
    mine, theirs, d_attn, bias_term = attention_backward(
        side, grad_branch, h_one, attn_full, attended, qkv, probs, cosine, sine
    )

    grad_h_one = mine + hop(theirs, "zl", 1).astype(F32)
    my_normed = own_rows(normed_one, zl)
    gain_one_term = jnp.sum(grad_h_one * my_normed, axis=0)
    grad_n_one = grad_h_one * norm_gain1
    grad_tokens = grad_resid + own_rows(factor_one, zl) * (
        grad_n_one - my_normed * jnp.mean(grad_n_one * my_normed, axis=-1, keepdims=True)
    )
    grad_tokens = both_rows(grad_tokens.astype(BF), zl).astype(F32)

    d_attn = scatter_attn(d_attn, spot)
    d_query, d_key = d_attn[0, :, : HEADS * HD], d_attn[0, :, HEADS * HD :]
    d_value, d_outproj = d_attn[1, :, :HD], d_attn[1, :, HD:]
    vectors = jnp.concatenate([gain_one_term, gain_two_term, bias_term[0]]).reshape(32, 128)
    vectors = sum_vectors(vectors, spot).reshape(-1)
    gain_one, gain_two, d_qbias, d_kbias, d_vbias = jnp.split(
        vectors, [1536, 3072, 3072 + HEADS * HD, 3072 + ATT]
    )
    return (
        mixed_out,
        grad_tokens,
        gain_one,
        d_query,
        d_qbias,
        d_key,
        d_kbias,
        d_value,
        d_vbias,
        d_outproj.T,
        gain_two,
        d_gate,
        d_up,
        d_down.T,
    )


def solution(mesh):
    split = Mesh(mesh.devices.reshape(4, 4, 2, 2, 2), EVERY)
    return jax.shard_map(
        on_device,
        mesh=split,
        in_specs=(
            P(WIDE, None),
            P(WIDE, None),
            P(),
            P(WIDE, "zl"),
            P("zl"),
            P(WIDE, "zl"),
            P("zl"),
            P(WIDE, "zl"),
            P("zl"),
            P("zl", WIDE),
            P(),
            P(WIDE, "zl"),
            P(WIDE, "zl"),
            P("zl", WIDE),
            P(WIDE, None),
        ),
        out_specs=(
            P(WIDE, None),
            P(WIDE, None),
            P(),
            P(WIDE, "zl"),
            P("zl"),
            P(WIDE, "zl"),
            P("zl"),
            P(WIDE, "zl"),
            P("zl"),
            P("zl", WIDE),
            P(),
            P(WIDE, "zl"),
            P(WIDE, "zl"),
            P("zl", WIDE),
        ),
        check_vma=False,
    )
```

```python
import functools

import jax
import jax.numpy as jnp
from jax import lax
from jax.experimental import pallas as pl
from jax.experimental.pallas import tpu as pltpu
from jax.sharding import Mesh, PartitionSpec as P

HD = 128
BF = jnp.bfloat16
F32 = jnp.float32
rope_base = 10000.0
norm_eps = 1e-06
WIDE = ("y", "x", "zh", "c")
EVERY = ("y", "x", "zh", "c", "zl")
SLICE = 1152
ATT = 896
HEADS = 6
STEPS = (0, 1, 3, 2)
BACK = (0, 2, 1, 3)
VEC = 16


def mm(left, right):
    return jnp.dot(left, right, preferred_element_type=F32)


def contract_rows(left, right):
    return lax.dot_general(left, right, (((0,), (0,)), ((), ())), preferred_element_type=F32)


def contract_cols(left, right):
    return lax.dot_general(left, right, (((1,), (1,)), ((), ())), preferred_element_type=F32)


def hop(value, axis, step=1):
    size = lax.axis_size(axis)
    return lax.ppermute(value, axis, [(i, (i + step) % size) for i in range(size)])


def zhop(value, step):
    return lax.ppermute(value, ("zh", "zl"), [(i, (i + step) % 4) for i in range(4)])


def plane_hop(value, step, turned):
    pairs = []
    for y in range(4):
        for x in range(4):
            for c in range(2):
                if c == turned:
                    to = (y, (x + step) % 4)
                else:
                    to = ((y + step) % 4, x)
                pairs.append(((y * 4 + x) * 2 + c, (to[0] * 4 + to[1]) * 2 + c))
    return lax.ppermute(value, ("y", "x", "c"), pairs)


def pair(mine, theirs, side, dim):
    first = jnp.where(side == 0, mine, theirs)
    second = jnp.where(side == 0, theirs, mine)
    return jnp.stack([first, second], dim)


def tie(*values):
    return lax.optimization_barrier(values)


def pick(value, index, dim=0):
    return lax.dynamic_index_in_dim(value, index, dim, keepdims=False)


def first_hops(attn, ffn, spot):
    zh, c = spot[2], spot[3]
    sent = [pick(attn, 1 - c)] + [pick(ffn[i], 1 - c) for i in range(2)]
    got = jnp.split(hop(jnp.concatenate(sent, 1), "c"), [ATT, ATT + 3 * SLICE], 1)
    attn = pair(pick(attn, c), got[0], c, 0).reshape(48, ATT)
    ffn = [pair(pick(ffn[i], c), got[1 + i], c, 0).reshape(48, 3 * SLICE) for i in range(2)]
    ffn = jnp.stack(ffn, 0)
    got = hop(jnp.concatenate([attn, pick(ffn, 1 - zh)], 1), "zh")
    attn = pair(attn, got[:, :ATT], zh, 0).reshape(96, ATT)
    return attn, pair(pick(ffn, zh), got[:, ATT:], zh, 0).reshape(96, 3 * SLICE)


def gather_attn(block):
    block = jnp.stack([block] + [plane_hop(block, k, 0) for k in STEPS[1:]], 0)
    pieces = [block] + [plane_hop(block, k, 1) for k in STEPS[1:]]
    return pieces, [hop(piece, "c") for piece in pieces]


def ring_sum(own, sent, turned):
    got = [plane_hop(value, k, turned).astype(F32) for k, value in zip(STEPS[1:], sent)]
    return (own.astype(F32) + got[2]) + (got[0] + got[1])


def trade(blocks, spot):
    me = spot[2] * 2 + spot[3]
    blocks = blocks.reshape((4,) + blocks.shape[2:])
    got = [pick(blocks, me)]
    for flip in (1, 2, 3):
        pairs = [(i, i ^ flip) for i in range(4)]
        got.append(lax.ppermute(pick(blocks, me ^ flip), ("zh", "c"), pairs))
    low = pair(got[0], got[1], spot[3], 0)
    return pair(low, pair(got[2], got[3], spot[3], 0), spot[2], 0)


def gather_tokens(value):
    pieces = [value] + [zhop(value, k) for k in STEPS[1:]]
    return pieces, [hop(piece, "c") for piece in pieces]


def sum_pieces(pieces):
    back, ahead, far = zhop(pieces[1], 3), zhop(pieces[2], 1), zhop(pieces[3], 2)
    return pieces[0].astype(F32) + far.astype(F32) + (back.astype(F32) + ahead.astype(F32))


def both_rows(mine, zl):
    return pair(mine, hop(mine, "zl"), zl, 0).reshape(2 * mine.shape[0], mine.shape[1])


def own_rows(value, side):
    half = value.shape[0] // 2
    return lax.dynamic_slice_in_dim(value, side * half, half, 0)


HBM = pl.BlockSpec(memory_space=pltpu.HBM)
VMEM = pl.BlockSpec(memory_space=pltpu.VMEM)
SMEM = pl.BlockSpec(memory_space=pltpu.SMEM)


def params(mib):
    return pltpu.CompilerParams(vmem_limit_bytes=mib * 2**20)


def cost(flops, moved, exps=0):
    return pl.CostEstimate(flops=flops, bytes_accessed=moved, transcendentals=exps)


def block_rows(spot, core, outer, inner):
    y, x = spot[0], spot[1]
    far, near = STEPS[outer], STEPS[inner]
    row = jnp.where(core == 0, (y - far) & 3, (y - near) & 3)
    col = jnp.where(core == 0, (x - near) & 3, (x - far) & 3)
    return pl.multiple_of((row * 4 + col) * 96, 96)


def load_weights(spot, pieces, w):
    for side in range(2):
        core = spot[3] if side == 0 else 1 - spot[3]
        for outer in range(4):
            for inner in range(4):
                row = block_rows(spot, core, outer, inner)
                w[core, pl.ds(row, 96)] = pieces[side * 4 + outer][inner]


def halves(side, value, mine_ref, theirs_ref):
    half = value.shape[0] // 2
    low, high = value[:half], value[half:]
    first = side == 0
    mine_ref[...] = jnp.where(first, low, high)
    theirs_ref[...] = jnp.where(first, high, low).astype(BF)


def turn(value, cosine, sine):
    return value * cosine + pltpu.roll(value, HD // 2, 1) * sine


def attention_kernel(spot, h, bias, cosine, sine, keep, *rest):
    pieces = rest[:8]
    mine, theirs, attended, qkv_out, probs_out, w = rest[8:]
    scale = HD ** (-0.5)
    load_weights(spot, pieces, w)
    cos, sin = cosine[...], sine[...]
    allowed = keep[...] > 0.5
    q_cols = HEADS * HD
    first = mm(h[...], w[0]) + bias[:, :ATT]
    keys = turn(first[:, q_cols:], cos, sin).astype(BF)
    values = (mm(h[...], w[1, :, :HD]) + bias[:, ATT:]).astype(BF)
    qkv_out[:, q_cols : q_cols + HD] = keys
    qkv_out[:, q_cols + HD :] = values
    for g in range(HEADS):
        cols = slice(g * HD, (g + 1) * HD)
        query = turn(first[:, cols], cos, sin).astype(BF)
        qkv_out[:, cols] = query
        logits = jnp.where(allowed, contract_cols(query, keys) * scale, -1000000000.0)
        expo = jnp.exp(logits - jnp.max(logits, axis=-1, keepdims=True))
        probs = expo / jnp.sum(expo, axis=-1, keepdims=True)
        probs_out[g] = probs
        attended[:, cols] = mm(probs.astype(BF), values).astype(BF)
    halves(spot[4], contract_cols(attended[...], w[1, :, HD:]), mine, theirs)


def attention_forward(spot, h, bias, cosine, sine, keep, pieces):
    rows, d = h.shape
    return pl.pallas_call(
        attention_kernel,
        in_specs=[SMEM] + [VMEM] * 13,
        out_shape=(
            jax.ShapeDtypeStruct((rows // 2, d), F32),
            jax.ShapeDtypeStruct((rows // 2, d), BF),
            jax.ShapeDtypeStruct((rows, HEADS * HD), BF),
            jax.ShapeDtypeStruct((rows, (HEADS + 2) * HD), BF),
            jax.ShapeDtypeStruct((HEADS, rows, rows), F32),
        ),
        scratch_shapes=[pltpu.VMEM((2, d, ATT), BF)],
        compiler_params=params(24),
        cost_estimate=cost(2_200_000_000, 12_000_000, 400_000),
        name="attention",
    )(spot, h, bias, cosine, sine, keep, *pieces)


def attention_back_kernel(
    spot, mine_in, theirs_in, h, tokens, factor, gain_two, attended, qkv, probs, cosine, sine, *rest
):
    pieces = rest[:8]
    mine, theirs, grads_mine, grads_theirs = rest[8:12]
    w, branch, grad_qkv, grads = rest[12:]
    scale = HD ** (-0.5)
    load_weights(spot, pieces, w)
    half, d = mine_in.shape
    zl = spot[4]
    branch[pl.ds(pl.multiple_of(zl * half, half), half)] = mine_in[...]
    branch[pl.ds(pl.multiple_of((1 - zl) * half, half), half)] = theirs_in[...]
    cos, sin = cosine[...], -sine[...]
    q_cols = HEADS * HD
    keys = qkv[:, q_cols : q_cols + HD]
    values = qkv[:, q_cols + HD :]
    grad_att = mm(branch[...], w[1, :, HD:]).astype(BF)
    grad_key = jnp.zeros((2 * half, HD), F32)
    grad_value = jnp.zeros((2 * half, HD), F32)
    for g in range(HEADS):
        cols = slice(g * HD, (g + 1) * HD)
        grad_head = grad_att[:, cols]
        grad_probs = contract_cols(grad_head, values)
        prob = probs[g]
        inner = jnp.sum(prob * grad_probs, axis=-1, keepdims=True)
        grad_logits = (prob * (grad_probs - inner)).astype(BF)
        grad_query = mm(grad_logits, keys) * scale
        grad_qkv[:, cols] = turn(grad_query, cos, sin).astype(BF)
        grad_key += contract_rows(grad_logits, qkv[:, cols])
        grad_value += contract_rows(prob.astype(BF), grad_head)
    grad_qkv[:, q_cols : q_cols + HD] = turn(grad_key * scale, cos, sin).astype(BF)
    grad_qkv[:, q_cols + HD :] = grad_value.astype(BF)
    grads[0] = contract_rows(h[...], grad_qkv[:, :ATT]).astype(BF)
    grads[1, :, :HD] = contract_rows(h[...], grad_qkv[:, ATT:]).astype(BF)
    grads[1, :, HD:] = contract_rows(branch[...], attended[...]).astype(BF)
    grad_h = contract_cols(grad_qkv[:, :ATT], w[0])
    grad_h += contract_cols(grad_qkv[:, ATT:], w[1, :, :HD])
    halves(zl, grad_h, mine, theirs)
    bias = jnp.sum(grad_qkv[...].astype(F32), axis=0, keepdims=True)
    gain_one = jnp.sum(grad_h * (tokens[...].astype(F32) * factor[...]), axis=0, keepdims=True)
    spare = jnp.zeros((1, ATT - q_cols), F32)
    lines = [gain_one[:, :q_cols], gain_one[:, q_cols:]]
    lines += [gain_two[:, :q_cols], gain_two[:, q_cols:], bias[:, :q_cols]]
    lines = [jnp.concatenate([line, spare], 1) for line in lines]
    lines.append(jnp.concatenate([bias[:, q_cols:], jnp.zeros((1, ATT - 2 * HD), F32)], 1))
    lines.append(jnp.zeros((VEC - 6, ATT), F32))
    vectors = jnp.concatenate(lines, 0).astype(BF)
    for side, out in enumerate((grads_mine, grads_theirs)):
        core = spot[3] if side == 0 else 1 - spot[3]
        for outer in range(4):
            for inner in range(4):
                row = block_rows(spot, core, BACK[outer], BACK[inner])
                out[outer, inner * 96 : inner * 96 + 96] = grads[core, pl.ds(row, 96)]
            out[outer, 4 * 96 :] = vectors


def attention_backward(
    spot, mine, theirs, h, tokens, factor, gain_two, attended, qkv, probs, cosine, sine, pieces
):
    rows, d = h.shape
    blocks = jax.ShapeDtypeStruct((4, 4 * 96 + VEC, ATT), BF)
    return pl.pallas_call(
        attention_back_kernel,
        in_specs=[SMEM] + [VMEM] * 19,
        out_shape=(
            jax.ShapeDtypeStruct((rows // 2, d), F32),
            jax.ShapeDtypeStruct((rows // 2, d), BF),
            blocks,
            blocks,
        ),
        scratch_shapes=[
            pltpu.VMEM((2, d, ATT), BF),
            pltpu.VMEM((rows, d), BF),
            pltpu.VMEM((rows, (HEADS + 2) * HD), BF),
            pltpu.VMEM((2, d, ATT), BF),
        ],
        compiler_params=params(32),
        cost_estimate=cost(4_300_000_000, 20_000_000),
        name="attention_back",
    )(spot, mine, theirs, h, tokens, factor, gain_two, attended, qkv, probs, cosine, sine, *pieces)


CHUNKS = [(start, min(256, SLICE - start)) for start in range(0, SLICE, 256)]


def block_places(zl):
    return zl, 3 * (1 - zl), 1 + zl, 2 + zl


def hidden_kernel(spot, h0, h1, h2, h3, g, w, h, act, sems):
    rows = h0.shape[0]
    copies = []
    for i, (place, piece) in enumerate(zip(block_places(spot[4]), (h0, h1, h2, h3))):
        target = h.at[pl.ds(pl.multiple_of(place * rows, rows), rows)]
        copies.append(pltpu.make_async_copy(piece, target, sems.at[i]))
    for copy in copies:
        copy.start()
    for copy in copies:
        copy.wait()
    for start, size in CHUNKS:
        cols = [slice(part * SLICE + start, part * SLICE + start + size) for part in range(3)]
        gate = mm(h[...], w[:, cols[0]])
        up_act = mm(h[...], w[:, cols[1]])
        grad = mm(g[...], w[:, cols[2]])
        sigma = jax.nn.sigmoid(gate)
        swish = gate * sigma
        act[:, cols[0]] = (grad * up_act * sigma * (1.0 + gate * (1.0 - sigma))).astype(BF)
        act[:, cols[1]] = (grad * swish).astype(BF)
        act[:, cols[2]] = (swish * up_act).astype(BF)


def hidden_act(spot, pieces, g, w):
    rows, d = g.shape
    return pl.pallas_call(
        hidden_kernel,
        in_specs=[SMEM] + [HBM] * 4 + [VMEM] * 2,
        out_specs=(VMEM, VMEM),
        out_shape=(
            jax.ShapeDtypeStruct((rows, d), BF),
            jax.ShapeDtypeStruct((rows, 3 * SLICE), BF),
        ),
        scratch_shapes=[pltpu.SemaphoreType.DMA((4,))],
        compiler_params=params(24),
        cost_estimate=cost(5_400_000_000, 20_000_000, 600_000),
        name="hidden",
    )(spot, *pieces, g, w)


def back_kernel(start, stop, act, w, out):
    for row in range(0, w.shape[0], 256):
        cols = slice(row, row + 256)
        out[:, cols] = contract_cols(act[:, start:stop], w[cols, : stop - start]).astype(BF)


def back_sum_kernel(start, stop, spot, act, w, other, out0, out1, out2, out3, part):
    rows = out0.shape[0]
    for row in range(0, w.shape[0], 256):
        cols = slice(row, row + 256)
        part[...] = contract_cols(act[:, start:stop], w[cols, : stop - start])
        part[...] += other[:, cols].astype(F32)
        for place, out in zip(block_places(spot[4]), (out0, out1, out2, out3)):
            block = pl.ds(pl.multiple_of(place * rows, rows), rows)
            out[:, cols] = part[block].astype(out.dtype)


def times_weights(start, stop, act, w, spot=None, other=None):
    rows, d = act.shape[0], w.shape[0]
    if other is None:
        shapes = pltpu.HBM((rows, d), BF)
        kernel, args, scratch = back_kernel, (act, w), []
    else:
        shapes = tuple(pltpu.HBM((rows // 4, d), F32 if i == 0 else BF) for i in range(4))
        kernel, args = back_sum_kernel, (spot, act, w, other)
        scratch = [pltpu.VMEM((rows, 256), F32)]
    return pl.pallas_call(
        functools.partial(kernel, start, stop),
        in_specs=[SMEM] * (len(args) - 2 - (other is not None)) + [VMEM] * (2 + (other is not None)),
        out_specs=jax.tree.map(lambda _: VMEM, shapes),
        out_shape=shapes,
        scratch_shapes=scratch,
        compiler_params=params(18),
        cost_estimate=cost(2 * rows * d * (stop - start), 10_000_000),
        name="hidden_back",
    )(*args)


def grad_hidden_input(act, w, *more):
    return times_weights(0, 2 * SLICE, act, w, *more)


def mixed_part(act, w, *more):
    return times_weights(2 * SLICE, 3 * SLICE, act, w, *more)


TILE = 256


def weights_kernel(h_mine, h_theirs, g_mine, g_theirs, act_mine, act_theirs, out, buf, sems):
    tiles = out.shape[0] // TILE

    def copy(at):
        row = pl.multiple_of(at * TILE, TILE)
        return pltpu.make_async_copy(buf.at[at & 1], out.at[pl.ds(row, TILE)], sems.at[at & 1])

    def body(step, _):
        @pl.when(step >= 2)
        def _():
            copy(step - 2).wait()

        rows = pl.ds(pl.multiple_of(step * TILE, TILE), TILE)
        for left, start, stop in ((0, 0, 2 * SLICE), (1, 2 * SLICE, 3 * SLICE)):
            mine, theirs = ((h_mine, h_theirs), (g_mine, g_theirs))[left]
            part = contract_rows(mine[:, rows], act_mine[:, start:stop])
            part += contract_rows(theirs[:, rows], act_theirs[:, start:stop])
            buf[step & 1, :, start:stop] = part.astype(BF)
        copy(step).start()
        return 0

    lax.fori_loop(0, tiles, body, 0)
    copy(tiles - 2).wait()
    copy(tiles - 1).wait()


def hidden_weights(h_mine, h_theirs, g_mine, g_theirs, act_mine, act_theirs):
    rows, d = h_mine.shape
    return pl.pallas_call(
        weights_kernel,
        in_specs=[VMEM] * 6,
        out_specs=HBM,
        out_shape=pltpu.HBM((d, 3 * SLICE), BF),
        scratch_shapes=[
            pltpu.VMEM((2, TILE, 3 * SLICE), BF),
            pltpu.SemaphoreType.DMA((2,)),
        ],
        compiler_params=params(18),
        cost_estimate=cost(10_900_000_000, 24_000_000),
        name="hidden_weights",
    )(h_mine, h_theirs, g_mine, g_theirs, act_mine, act_theirs)


def doc_layout(lengths, count):
    ends = jnp.cumsum(lengths)
    starts = ends - lengths
    place = jnp.arange(count, dtype=jnp.int32)
    segment = jnp.sum((place[:, None] >= ends[None, :]).astype(jnp.int32), axis=1)
    labels = jnp.arange(lengths.shape[0], dtype=jnp.int32)
    first = jnp.sum(jnp.where(segment[:, None] == labels[None, :], starts[None, :], 0), axis=1)
    return (segment, place - first, place)


def on_device(
    tokens,
    doc_lengths,
    norm_gain1,
    w_query,
    b_query,
    w_key,
    b_key,
    w_value,
    b_value,
    w_out,
    norm_gain2,
    w_gate,
    w_up,
    w_down,
    out_grad,
):
    spot = tuple(lax.axis_index(axis) for axis in EVERY)
    y, x, zh, c, zl = spot
    place_of = jnp.stack(spot)
    rows, d = tokens.shape
    hidden_units = w_gate.shape[1]
    pad = 4 * SLICE - hidden_units
    q_cols = HEADS * HD

    attn = jnp.concatenate([w_query, w_key, w_value, w_out.T], 1)
    attn = jnp.stack([attn[:, :ATT], attn[:, ATT:]], 0)
    ffn = jnp.stack([w_gate, w_up, w_down.T], 1)
    ffn = jnp.pad(ffn, ((0, 0), (0, 0), (0, pad))).reshape(24, 3, 4, SLICE)
    ffn = ffn.transpose(2, 0, 1, 3).reshape(2, 2, 24, 3 * SLICE)
    segment, position, place = doc_layout(doc_lengths[0], rows)
    inverse = rope_base ** (-jnp.arange(0, HD, 2, dtype=F32) / HD)
    angle = position.astype(F32)[:, None] * inverse[None, :]
    cosine, sine = jnp.cos(angle), jnp.sin(angle)
    cosine = jnp.concatenate([cosine, cosine], 1)
    sine = jnp.concatenate([-sine, sine], 1)
    keep = (segment[:, None] == segment[None, :]) & (place[None, :] <= place[:, None])
    inputs = tokens.astype(F32)
    factor_one = lax.rsqrt(jnp.mean(inputs * inputs, axis=-1, keepdims=True) + norm_eps)
    normed_one = inputs * factor_one
    h_one = (normed_one * norm_gain1).astype(BF)
    bias = jnp.concatenate([b_query, b_key, b_value])[None]
    attn, ffn = first_hops(attn, ffn, spot)
    ffn_full = lax.all_gather(ffn, ("y", "x"), axis=0, tiled=True)
    attn, h_one, cosine, sine, keep = tie(attn, h_one, cosine, sine, keep.astype(F32))
    far = hop(out_grad, "zh")
    near_theirs, far_theirs = hop(out_grad, "c"), hop(far, "c")
    mine, theirs = gather_attn(attn)
    pieces, far, near_theirs, far_theirs = tie(mine + theirs, far, near_theirs, far_theirs)

    mine, theirs, attended, qkv, probs = attention_forward(
        place_of, h_one, bias, cosine, sine, keep, pieces
    )
    theirs, far, near_theirs, far_theirs = tie(theirs, far, near_theirs, far_theirs)
    grad_mine = jnp.concatenate([out_grad, far], 0)
    grad_theirs = jnp.concatenate([near_theirs, far_theirs], 0)
    theirs, grad_mine, grad_theirs = tie(hop(theirs, "zl"), grad_mine, grad_theirs)
    resid = own_rows(tokens, zl).astype(F32) + mine + theirs.astype(F32)

    factor_two = lax.rsqrt(jnp.mean(resid * resid, axis=-1, keepdims=True) + norm_eps)
    normed_two = resid * factor_two
    h_two = (normed_two * norm_gain2).astype(BF)
    mine = [h_two] + [zhop(h_two, k) for k in STEPS[1:]]
    first, ffn_full = tie(hop(h_two, "c"), ffn_full)
    theirs = [first] + [hop(piece, "c") for piece in mine[1:]]
    h_mine, act_mine = hidden_act(place_of, mine, grad_mine, ffn_full)
    h_theirs, act_theirs = hidden_act(place_of, theirs, grad_theirs, ffn_full)
    back = hop(grad_hidden_input(act_theirs, ffn_full), "c")
    back = grad_hidden_input(act_mine, ffn_full, place_of, back)
    back, act_mine, act_theirs = tie(back, act_mine, act_theirs)
    d_ffn = hidden_weights(h_mine, h_theirs, grad_mine, grad_theirs, act_mine, act_theirs)
    d_ffn, grad_h_two, act_mine, act_theirs = tie(d_ffn, sum_pieces(back), act_mine, act_theirs)
    d_ffn = lax.psum_scatter(d_ffn, ("y", "x"), scatter_dimension=0, tiled=True)

    gain_two = jnp.sum(grad_h_two * normed_two, axis=0, keepdims=True)
    grad_n_two = grad_h_two * norm_gain2
    grad_resid = own_rows(out_grad, zl).astype(F32) + factor_two * (
        grad_n_two - normed_two * jnp.mean(grad_n_two * normed_two, axis=-1, keepdims=True)
    )
    grad_branch, act_mine, act_theirs = tie(grad_resid.astype(BF), act_mine, act_theirs)
    down_full = ffn_full[:, 2 * SLICE :]
    mixed = hop(mixed_part(act_theirs, down_full), "c")
    mixed = mixed_part(act_mine, down_full, place_of, mixed)
    branch_theirs, mixed = tie(hop(grad_branch, "zl"), mixed)
    mixed = (resid + sum_pieces(mixed)).astype(BF)

    mine, theirs, grads_mine, grads_theirs = attention_backward(
        place_of,
        grad_branch,
        branch_theirs,
        h_one,
        tokens,
        factor_one,
        gain_two,
        attended,
        qkv,
        probs,
        cosine,
        sine,
        pieces,
    )
    grads_theirs = hop(grads_theirs, "c")
    grad_h_one = mine + hop(theirs, "zl").astype(F32)
    my_normed = own_rows(normed_one, zl)
    grad_n_one = grad_h_one * norm_gain1
    grad_tokens = grad_resid + own_rows(factor_one, zl) * (
        grad_n_one - my_normed * jnp.mean(grad_n_one * my_normed, axis=-1, keepdims=True)
    )
    grad_tokens = grad_tokens.astype(BF)

    parts = [(grads_mine[p].astype(F32) + grads_theirs[p].astype(F32)).astype(BF) for p in range(4)]
    part = ring_sum(parts[0], parts[1:], 1).astype(BF)
    part, mixed, grad_tokens = tie(part, mixed, grad_tokens)
    extra = part[4 * 96 :]
    parts = [jnp.concatenate([part[p * 96 : p * 96 + 96], extra], 0) for p in range(4)]
    part = ring_sum(parts[0], parts[1:], 0)
    mixed_out = both_rows(mixed, zl)
    grad_tokens = both_rows(grad_tokens, zl).astype(F32)
    rows, extra = part[:96].reshape(2, 48, ATT), part[96:].astype(BF)
    got = hop(jnp.concatenate([pick(rows, 1 - zh).astype(BF), extra], 0), "zh").astype(F32)
    got, mixed_out, grad_tokens, d_ffn = tie(got, mixed_out, grad_tokens, d_ffn)
    d_ffn = trade(d_ffn.reshape(2, 2, 24, 3 * SLICE), spot).astype(F32)
    rows = (pick(rows, zh) + got[:48]).reshape(2, 24, ATT)
    extra = (extra.astype(F32) + got[48:]).astype(BF)
    got = hop(jnp.concatenate([pick(rows, 1 - c).astype(BF), extra], 0), "c").astype(F32)
    sums = (extra.astype(F32) + got[24:]) * 0.5
    d_attn = pair(pick(rows, c), got[:24], c, 0)
    d_query, d_key = d_attn[0, :, :q_cols], d_attn[0, :, q_cols:]
    d_value, d_outproj = d_attn[1, :, :HD], d_attn[1, :, HD:]
    gains = sums[:4, :q_cols].astype(BF)
    gains = (gains.astype(F32) + hop(gains, "zl").astype(F32)).reshape(2, d)
    d_ffn = d_ffn.reshape(4, 24, 3, SLICE).transpose(2, 1, 0, 3).reshape(3, 24, 4 * SLICE)
    d_gate, d_up, d_down = (d_ffn[i, :, :hidden_units] for i in range(3))
    return (
        mixed_out,
        grad_tokens,
        gains[0],
        d_query,
        sums[4, :q_cols],
        d_key,
        sums[5, :HD],
        d_value,
        sums[5, HD : 2 * HD],
        d_outproj.T,
        gains[1],
        d_gate,
        d_up,
        d_down.T,
    )


def solution(mesh):
    split = Mesh(mesh.devices.reshape(4, 4, 2, 2, 2), EVERY)
    return jax.shard_map(
        on_device,
        mesh=split,
        in_specs=(
            P(WIDE, None),
            P(WIDE, None),
            P(),
            P(WIDE, "zl"),
            P("zl"),
            P(WIDE, "zl"),
            P("zl"),
            P(WIDE, "zl"),
            P("zl"),
            P("zl", WIDE),
            P(),
            P(WIDE, "zl"),
            P(WIDE, "zl"),
            P("zl", WIDE),
            P(WIDE, None),
        ),
        out_specs=(
            P(WIDE, None),
            P(WIDE, None),
            P(),
            P(WIDE, "zl"),
            P("zl"),
            P(WIDE, "zl"),
            P("zl"),
            P(WIDE, "zl"),
            P("zl"),
            P("zl", WIDE),
            P(),
            P(WIDE, "zl"),
            P(WIDE, "zl"),
            P("zl", WIDE),
        ),
        check_vma=False,
    )
```

```python
import functools

import jax
import jax.numpy as jnp
from jax import lax
from jax.experimental import pallas as pl
from jax.experimental.pallas import tpu as pltpu
from jax.sharding import Mesh, PartitionSpec as P

HD = 128
BF = jnp.bfloat16
F32 = jnp.float32
rope_base = 10000.0
norm_eps = 1e-06
WIDE = ("y", "x", "zh", "c")
EVERY = ("y", "x", "zh", "c", "zl")
SLICE = 1152
ATT = 896
HEADS = 6
STEPS = (0, 1, 3, 2)
BACK = (0, 2, 1, 3)
VEC = 16


def mm(left, right):
    return jnp.dot(left, right, preferred_element_type=F32)


def contract_rows(left, right):
    return lax.dot_general(left, right, (((0,), (0,)), ((), ())), preferred_element_type=F32)


def contract_cols(left, right):
    return lax.dot_general(left, right, (((1,), (1,)), ((), ())), preferred_element_type=F32)


def hop(value, axis, step=1):
    size = lax.axis_size(axis)
    return lax.ppermute(value, axis, [(i, (i + step) % size) for i in range(size)])


def zhop(value, step):
    return lax.ppermute(value, ("zh", "zl"), [(i, (i + step) % 4) for i in range(4)])


def plane_hop(value, step, turned):
    pairs = []
    for y in range(4):
        for x in range(4):
            for c in range(2):
                if c == turned:
                    to = (y, (x + step) % 4)
                else:
                    to = ((y + step) % 4, x)
                pairs.append(((y * 4 + x) * 2 + c, (to[0] * 4 + to[1]) * 2 + c))
    return lax.ppermute(value, ("y", "x", "c"), pairs)


def pair(mine, theirs, side, dim):
    first = jnp.where(side == 0, mine, theirs)
    second = jnp.where(side == 0, theirs, mine)
    return jnp.stack([first, second], dim)


def tie(*values):
    return lax.optimization_barrier(values)


def pick(value, index, dim=0):
    return lax.dynamic_index_in_dim(value, index, dim, keepdims=False)


def first_hops(attn, ffn, spot):
    zh, c = spot[2], spot[3]
    ffn = trade(ffn, spot).reshape(96, 3 * SLICE)
    attn = pair(pick(attn, c), hop(pick(attn, 1 - c), "c"), c, 0).reshape(48, ATT)
    return pair(attn, hop(attn, "zh"), zh, 0).reshape(96, ATT), ffn


def gather_attn(block):
    block = jnp.stack([block] + [plane_hop(block, k, 0) for k in STEPS[1:]], 0)
    pieces = [block] + [plane_hop(block, k, 1) for k in STEPS[1:]]
    return pieces, [hop(piece, "c") for piece in pieces]


def ring_sum(own, sent, turned):
    got = [plane_hop(value, k, turned).astype(F32) for k, value in zip(STEPS[1:], sent)]
    return (own.astype(F32) + got[2]) + (got[0] + got[1])


def trade(blocks, spot):
    me = spot[2] * 2 + spot[3]
    blocks = blocks.reshape((4,) + blocks.shape[2:])
    got = [pick(blocks, me)]
    for flip in (1, 2, 3):
        pairs = [(i, i ^ flip) for i in range(4)]
        got.append(lax.ppermute(pick(blocks, me ^ flip), ("zh", "c"), pairs))
    low = pair(got[0], got[1], spot[3], 0)
    return pair(low, pair(got[2], got[3], spot[3], 0), spot[2], 0)


def gather_tokens(value):
    pieces = [value] + [zhop(value, k) for k in STEPS[1:]]
    return pieces, [hop(piece, "c") for piece in pieces]


def send_pieces(pieces):
    return [pieces[0]] + [zhop(value, -k % 4) for k, value in zip(STEPS[1:], pieces[1:])]


def sum_pieces(pieces):
    back, ahead, far = (piece.astype(F32) for piece in pieces[1:])
    return pieces[0].astype(F32) + far + (back + ahead)


def both_rows(mine, zl):
    return pair(mine, hop(mine, "zl"), zl, 0).reshape(2 * mine.shape[0], mine.shape[1])


def own_rows(value, side):
    half = value.shape[0] // 2
    return lax.dynamic_slice_in_dim(value, side * half, half, 0)


HBM = pl.BlockSpec(memory_space=pltpu.HBM)
VMEM = pl.BlockSpec(memory_space=pltpu.VMEM)
SMEM = pl.BlockSpec(memory_space=pltpu.SMEM)


def params(mib):
    return pltpu.CompilerParams(vmem_limit_bytes=mib * 2**20)


def cost(flops, moved, exps=0):
    return pl.CostEstimate(flops=flops, bytes_accessed=moved, transcendentals=exps)


def block_rows(spot, core, outer, inner):
    y, x = spot[0], spot[1]
    far, near = STEPS[outer], STEPS[inner]
    row = jnp.where(core == 0, (y - far) & 3, (y - near) & 3)
    col = jnp.where(core == 0, (x - near) & 3, (x - far) & 3)
    return pl.multiple_of((row * 4 + col) * 96, 96)


def load_weights(spot, pieces, w):
    for side in range(2):
        core = spot[3] if side == 0 else 1 - spot[3]
        for outer in range(4):
            for inner in range(4):
                row = block_rows(spot, core, outer, inner)
                w[core, pl.ds(row, 96)] = pieces[side * 4 + outer][inner]


def halves(side, value, mine_ref, theirs_ref):
    half = value.shape[0] // 2
    low, high = value[:half], value[half:]
    first = side == 0
    mine_ref[...] = jnp.where(first, low, high)
    theirs_ref[...] = jnp.where(first, high, low).astype(BF)


def turn(value, cosine, sine):
    return value * cosine + pltpu.roll(value, HD // 2, 1) * sine


def attention_kernel(spot, h, bias, cosine, sine, keep, *rest):
    pieces = rest[:8]
    mine, theirs, attended, qkv_out, probs_out, w = rest[8:]
    scale = HD ** (-0.5)
    load_weights(spot, pieces, w)
    cos, sin = cosine[...], sine[...]
    allowed = keep[...] > 0.5
    q_cols = HEADS * HD
    first = mm(h[...], w[0]) + bias[:, :ATT]
    keys = turn(first[:, q_cols:], cos, sin).astype(BF)
    values = (mm(h[...], w[1, :, :HD]) + bias[:, ATT:]).astype(BF)
    qkv_out[:, q_cols : q_cols + HD] = keys
    qkv_out[:, q_cols + HD :] = values
    for g in range(HEADS):
        cols = slice(g * HD, (g + 1) * HD)
        query = turn(first[:, cols], cos, sin).astype(BF)
        qkv_out[:, cols] = query
        logits = jnp.where(allowed, contract_cols(query, keys) * scale, -1000000000.0)
        expo = jnp.exp(logits - jnp.max(logits, axis=-1, keepdims=True))
        probs = expo / jnp.sum(expo, axis=-1, keepdims=True)
        probs_out[g] = probs
        attended[:, cols] = mm(probs.astype(BF), values).astype(BF)
    halves(spot[4], contract_cols(attended[...], w[1, :, HD:]), mine, theirs)


def attention_forward(spot, h, bias, cosine, sine, keep, pieces):
    rows, d = h.shape
    return pl.pallas_call(
        attention_kernel,
        in_specs=[SMEM] + [VMEM] * 13,
        out_shape=(
            jax.ShapeDtypeStruct((rows // 2, d), F32),
            jax.ShapeDtypeStruct((rows // 2, d), BF),
            jax.ShapeDtypeStruct((rows, HEADS * HD), BF),
            jax.ShapeDtypeStruct((rows, (HEADS + 2) * HD), BF),
            jax.ShapeDtypeStruct((HEADS, rows, rows), F32),
        ),
        scratch_shapes=[pltpu.VMEM((2, d, ATT), BF)],
        compiler_params=params(24),
        cost_estimate=cost(2_200_000_000, 12_000_000, 400_000),
        name="attention",
    )(spot, h, bias, cosine, sine, keep, *pieces)


def attention_back_kernel(
    spot, mine_in, theirs_in, h, tokens, factor, gain_two, attended, qkv, probs, cosine, sine, *rest
):
    pieces = rest[:8]
    mine, theirs, grads_mine, grads_theirs = rest[8:12]
    w, branch, grad_qkv, grads = rest[12:]
    scale = HD ** (-0.5)
    load_weights(spot, pieces, w)
    half, d = mine_in.shape
    zl = spot[4]
    branch[pl.ds(pl.multiple_of(zl * half, half), half)] = mine_in[...]
    branch[pl.ds(pl.multiple_of((1 - zl) * half, half), half)] = theirs_in[...]
    cos, sin = cosine[...], -sine[...]
    q_cols = HEADS * HD
    keys = qkv[:, q_cols : q_cols + HD]
    values = qkv[:, q_cols + HD :]
    grad_att = mm(branch[...], w[1, :, HD:]).astype(BF)
    grad_key = jnp.zeros((2 * half, HD), F32)
    grad_value = jnp.zeros((2 * half, HD), F32)
    for g in range(HEADS):
        cols = slice(g * HD, (g + 1) * HD)
        grad_head = grad_att[:, cols]
        grad_probs = contract_cols(grad_head, values)
        prob = probs[g]
        inner = jnp.sum(prob * grad_probs, axis=-1, keepdims=True)
        grad_logits = (prob * (grad_probs - inner)).astype(BF)
        grad_query = mm(grad_logits, keys) * scale
        grad_qkv[:, cols] = turn(grad_query, cos, sin).astype(BF)
        grad_key += contract_rows(grad_logits, qkv[:, cols])
        grad_value += contract_rows(prob.astype(BF), grad_head)
    grad_qkv[:, q_cols : q_cols + HD] = turn(grad_key * scale, cos, sin).astype(BF)
    grad_qkv[:, q_cols + HD :] = grad_value.astype(BF)
    grads[0] = contract_rows(h[...], grad_qkv[:, :ATT]).astype(BF)
    grads[1, :, :HD] = contract_rows(h[...], grad_qkv[:, ATT:]).astype(BF)
    grads[1, :, HD:] = contract_rows(branch[...], attended[...]).astype(BF)
    grad_h = contract_cols(grad_qkv[:, :ATT], w[0])
    grad_h += contract_cols(grad_qkv[:, ATT:], w[1, :, :HD])
    halves(zl, grad_h, mine, theirs)
    bias = jnp.sum(grad_qkv[...].astype(F32), axis=0, keepdims=True)
    gain_one = jnp.sum(grad_h * (tokens[...].astype(F32) * factor[...]), axis=0, keepdims=True)
    spare = jnp.zeros((1, ATT - q_cols), F32)
    lines = [gain_one[:, :q_cols], gain_one[:, q_cols:]]
    lines += [gain_two[:, :q_cols], gain_two[:, q_cols:], bias[:, :q_cols]]
    lines = [jnp.concatenate([line, spare], 1) for line in lines]
    lines.append(jnp.concatenate([bias[:, q_cols:], jnp.zeros((1, ATT - 2 * HD), F32)], 1))
    lines.append(jnp.zeros((VEC - 6, ATT), F32))
    vectors = jnp.concatenate(lines, 0).astype(BF)
    for side, out in enumerate((grads_mine, grads_theirs)):
        core = spot[3] if side == 0 else 1 - spot[3]
        for outer in range(4):
            for inner in range(4):
                row = block_rows(spot, core, BACK[outer], BACK[inner])
                out[outer, inner * 96 : inner * 96 + 96] = grads[core, pl.ds(row, 96)]
            out[outer, 4 * 96 :] = vectors


def attention_backward(
    spot, mine, theirs, h, tokens, factor, gain_two, attended, qkv, probs, cosine, sine, pieces
):
    rows, d = h.shape
    blocks = jax.ShapeDtypeStruct((4, 4 * 96 + VEC, ATT), BF)
    return pl.pallas_call(
        attention_back_kernel,
        in_specs=[SMEM] + [VMEM] * 19,
        out_shape=(
            jax.ShapeDtypeStruct((rows // 2, d), F32),
            jax.ShapeDtypeStruct((rows // 2, d), BF),
            blocks,
            blocks,
        ),
        scratch_shapes=[
            pltpu.VMEM((2, d, ATT), BF),
            pltpu.VMEM((rows, d), BF),
            pltpu.VMEM((rows, (HEADS + 2) * HD), BF),
            pltpu.VMEM((2, d, ATT), BF),
        ],
        compiler_params=params(32),
        cost_estimate=cost(4_300_000_000, 20_000_000),
        name="attention_back",
    )(spot, mine, theirs, h, tokens, factor, gain_two, attended, qkv, probs, cosine, sine, *pieces)


CHUNKS = [(start, min(256, SLICE - start)) for start in range(0, SLICE, 256)]


def block_places(zl):
    return zl, 3 * (1 - zl), 1 + zl, 2 + zl


def hidden_kernel(spot, h0, h1, h2, h3, g, w, h, act, sems):
    rows = h0.shape[0]
    copies = []
    for i, (place, piece) in enumerate(zip(block_places(spot[4]), (h0, h1, h2, h3))):
        target = h.at[pl.ds(pl.multiple_of(place * rows, rows), rows)]
        copies.append(pltpu.make_async_copy(piece, target, sems.at[i]))
    for copy in copies:
        copy.start()
    for copy in copies:
        copy.wait()
    for start, size in CHUNKS:
        cols = [slice(part * SLICE + start, part * SLICE + start + size) for part in range(3)]
        gate = mm(h[...], w[:, cols[0]])
        up_act = mm(h[...], w[:, cols[1]])
        grad = mm(g[...], w[:, cols[2]])
        sigma = jax.nn.sigmoid(gate)
        swish = gate * sigma
        act[:, cols[0]] = (grad * up_act * sigma * (1.0 + gate * (1.0 - sigma))).astype(BF)
        act[:, cols[1]] = (grad * swish).astype(BF)
        act[:, cols[2]] = (swish * up_act).astype(BF)


def hidden_act(spot, pieces, g, w):
    rows, d = g.shape
    return pl.pallas_call(
        hidden_kernel,
        in_specs=[SMEM] + [HBM] * 4 + [VMEM] * 2,
        out_specs=(VMEM, VMEM),
        out_shape=(
            jax.ShapeDtypeStruct((rows, d), BF),
            jax.ShapeDtypeStruct((rows, 3 * SLICE), BF),
        ),
        scratch_shapes=[pltpu.SemaphoreType.DMA((4,))],
        compiler_params=params(24),
        cost_estimate=cost(5_400_000_000, 20_000_000, 600_000),
        name="hidden",
    )(spot, *pieces, g, w)


def back_kernel(start, stop, act, w, out):
    for row in range(0, w.shape[0], 256):
        cols = slice(row, row + 256)
        out[:, cols] = contract_cols(act[:, start:stop], w[cols, : stop - start]).astype(BF)


def back_sum_kernel(start, stop, spot, act, w, other, out0, out1, out2, out3, part):
    rows = out0.shape[0]
    for row in range(0, w.shape[0], 256):
        cols = slice(row, row + 256)
        part[...] = contract_cols(act[:, start:stop], w[cols, : stop - start])
        part[...] += other[:, cols].astype(F32)
        for place, out in zip(block_places(spot[4]), (out0, out1, out2, out3)):
            block = pl.ds(pl.multiple_of(place * rows, rows), rows)
            out[:, cols] = part[block].astype(out.dtype)


def times_weights(start, stop, act, w, spot=None, other=None):
    rows, d = act.shape[0], w.shape[0]
    if other is None:
        shapes = pltpu.HBM((rows, d), BF)
        kernel, args, scratch = back_kernel, (act, w), []
    else:
        shapes = tuple(pltpu.HBM((rows // 4, d), F32 if i == 0 else BF) for i in range(4))
        kernel, args = back_sum_kernel, (spot, act, w, other)
        scratch = [pltpu.VMEM((rows, 256), F32)]
    return pl.pallas_call(
        functools.partial(kernel, start, stop),
        in_specs=[SMEM] * (len(args) - 2 - (other is not None)) + [VMEM] * (2 + (other is not None)),
        out_specs=jax.tree.map(lambda _: VMEM, shapes),
        out_shape=shapes,
        scratch_shapes=scratch,
        compiler_params=params(18),
        cost_estimate=cost(2 * rows * d * (stop - start), 10_000_000),
        name="hidden_back",
    )(*args)


def grad_hidden_input(act, w, *more):
    return times_weights(0, 2 * SLICE, act, w, *more)


def mixed_part(act, w, *more):
    return times_weights(2 * SLICE, 3 * SLICE, act, w, *more)


TILE = 256


def weights_kernel(h_mine, h_theirs, g_mine, g_theirs, act_mine, act_theirs, out, buf, sems):
    tiles = out.shape[0] // TILE

    def copy(at):
        row = pl.multiple_of(at * TILE, TILE)
        return pltpu.make_async_copy(buf.at[at & 1], out.at[pl.ds(row, TILE)], sems.at[at & 1])

    def body(step, _):
        @pl.when(step >= 2)
        def _():
            copy(step - 2).wait()

        rows = pl.ds(pl.multiple_of(step * TILE, TILE), TILE)
        for left, start, stop in ((0, 0, 2 * SLICE), (1, 2 * SLICE, 3 * SLICE)):
            mine, theirs = ((h_mine, h_theirs), (g_mine, g_theirs))[left]
            part = contract_rows(mine[:, rows], act_mine[:, start:stop])
            part += contract_rows(theirs[:, rows], act_theirs[:, start:stop])
            buf[step & 1, :, start:stop] = part.astype(BF)
        copy(step).start()
        return 0

    lax.fori_loop(0, tiles, body, 0)
    copy(tiles - 2).wait()
    copy(tiles - 1).wait()


def hidden_weights(h_mine, h_theirs, g_mine, g_theirs, act_mine, act_theirs):
    rows, d = h_mine.shape
    return pl.pallas_call(
        weights_kernel,
        in_specs=[VMEM] * 6,
        out_specs=HBM,
        out_shape=pltpu.HBM((d, 3 * SLICE), BF),
        scratch_shapes=[
            pltpu.VMEM((2, TILE, 3 * SLICE), BF),
            pltpu.SemaphoreType.DMA((2,)),
        ],
        compiler_params=params(18),
        cost_estimate=cost(10_900_000_000, 24_000_000),
        name="hidden_weights",
    )(h_mine, h_theirs, g_mine, g_theirs, act_mine, act_theirs)


def doc_layout(lengths, count):
    ends = jnp.cumsum(lengths)
    starts = ends - lengths
    place = jnp.arange(count, dtype=jnp.int32)
    segment = jnp.sum((place[:, None] >= ends[None, :]).astype(jnp.int32), axis=1)
    labels = jnp.arange(lengths.shape[0], dtype=jnp.int32)
    first = jnp.sum(jnp.where(segment[:, None] == labels[None, :], starts[None, :], 0), axis=1)
    return (segment, place - first, place)


def on_device(
    tokens,
    doc_lengths,
    norm_gain1,
    w_query,
    b_query,
    w_key,
    b_key,
    w_value,
    b_value,
    w_out,
    norm_gain2,
    w_gate,
    w_up,
    w_down,
    out_grad,
):
    spot = tuple(lax.axis_index(axis) for axis in EVERY)
    y, x, zh, c, zl = spot
    place_of = jnp.stack(spot)
    rows, d = tokens.shape
    hidden_units = w_gate.shape[1]
    pad = 4 * SLICE - hidden_units
    q_cols = HEADS * HD

    attn = jnp.concatenate([w_query, w_key, w_value, w_out.T], 1)
    attn = jnp.stack([attn[:, :ATT], attn[:, ATT:]], 0)
    ffn = jnp.stack([w_gate, w_up, w_down.T], 1)
    ffn = jnp.pad(ffn, ((0, 0), (0, 0), (0, pad))).reshape(24, 3, 4, SLICE)
    ffn = ffn.transpose(2, 0, 1, 3).reshape(2, 2, 24, 3 * SLICE)
    segment, position, place = doc_layout(doc_lengths[0], rows)
    inverse = rope_base ** (-jnp.arange(0, HD, 2, dtype=F32) / HD)
    angle = position.astype(F32)[:, None] * inverse[None, :]
    cosine, sine = jnp.cos(angle), jnp.sin(angle)
    cosine = jnp.concatenate([cosine, cosine], 1)
    sine = jnp.concatenate([-sine, sine], 1)
    keep = (segment[:, None] == segment[None, :]) & (place[None, :] <= place[:, None])
    inputs = tokens.astype(F32)
    factor_one = lax.rsqrt(jnp.mean(inputs * inputs, axis=-1, keepdims=True) + norm_eps)
    normed_one = inputs * factor_one
    h_one = (normed_one * norm_gain1).astype(BF)
    bias = jnp.concatenate([b_query, b_key, b_value])[None]
    attn, ffn = first_hops(attn, ffn, spot)
    ffn_full = lax.all_gather(ffn, ("y", "x"), axis=0, tiled=True)
    attn, h_one, cosine, sine, keep = tie(attn, h_one, cosine, sine, keep.astype(F32))
    far = hop(out_grad, "zh")
    near_theirs, far_theirs = hop(out_grad, "c"), hop(far, "c")
    mine, theirs = gather_attn(attn)
    pieces, far, near_theirs, far_theirs = tie(mine + theirs, far, near_theirs, far_theirs)

    mine, theirs, attended, qkv, probs = attention_forward(
        place_of, h_one, bias, cosine, sine, keep, pieces
    )
    theirs, far, near_theirs, far_theirs = tie(theirs, far, near_theirs, far_theirs)
    grad_mine = jnp.concatenate([out_grad, far], 0)
    grad_theirs = jnp.concatenate([near_theirs, far_theirs], 0)
    theirs, grad_mine, grad_theirs = tie(hop(theirs, "zl"), grad_mine, grad_theirs)
    resid = own_rows(tokens, zl).astype(F32) + mine + theirs.astype(F32)

    factor_two = lax.rsqrt(jnp.mean(resid * resid, axis=-1, keepdims=True) + norm_eps)
    normed_two = resid * factor_two
    h_two = (normed_two * norm_gain2).astype(BF)
    mine = [h_two] + [zhop(h_two, k) for k in STEPS[1:]]
    mine[1], ffn_full = tie(mine[1], ffn_full)
    theirs = [hop(piece, "c") for piece in mine]
    h_mine, act_mine = hidden_act(place_of, mine, grad_mine, ffn_full)
    h_theirs, act_theirs = hidden_act(place_of, theirs, grad_theirs, ffn_full)
    back = hop(grad_hidden_input(act_theirs, ffn_full), "c")
    back = grad_hidden_input(act_mine, ffn_full, place_of, back)
    back, act_mine, act_theirs = tie(back, act_mine, act_theirs)
    d_ffn = hidden_weights(h_mine, h_theirs, grad_mine, grad_theirs, act_mine, act_theirs)
    d_ffn, back, act_mine, act_theirs = tie(d_ffn, send_pieces(back), act_mine, act_theirs)
    grad_h_two = sum_pieces(back)
    d_ffn = lax.psum_scatter(d_ffn, ("y", "x"), scatter_dimension=0, tiled=True)

    gain_two = jnp.sum(grad_h_two * normed_two, axis=0, keepdims=True)
    grad_n_two = grad_h_two * norm_gain2
    grad_resid = own_rows(out_grad, zl).astype(F32) + factor_two * (
        grad_n_two - normed_two * jnp.mean(grad_n_two * normed_two, axis=-1, keepdims=True)
    )
    grad_branch, act_mine, act_theirs = tie(grad_resid.astype(BF), act_mine, act_theirs)
    down_full = ffn_full[:, 2 * SLICE :]
    mixed = hop(mixed_part(act_theirs, down_full), "c")
    mixed = mixed_part(act_mine, down_full, place_of, mixed)
    branch_theirs, mixed = tie(hop(grad_branch, "zl"), mixed)
    mixed = (resid + sum_pieces(send_pieces(mixed))).astype(BF)

    mine, theirs, grads_mine, grads_theirs = attention_backward(
        place_of,
        grad_branch,
        branch_theirs,
        h_one,
        tokens,
        factor_one,
        gain_two,
        attended,
        qkv,
        probs,
        cosine,
        sine,
        pieces,
    )
    grads_theirs = hop(grads_theirs, "c")
    grad_h_one = mine + hop(theirs, "zl").astype(F32)
    my_normed = own_rows(normed_one, zl)
    grad_n_one = grad_h_one * norm_gain1
    grad_tokens = grad_resid + own_rows(factor_one, zl) * (
        grad_n_one - my_normed * jnp.mean(grad_n_one * my_normed, axis=-1, keepdims=True)
    )
    grad_tokens = grad_tokens.astype(BF)

    parts = [(grads_mine[p].astype(F32) + grads_theirs[p].astype(F32)).astype(BF) for p in range(4)]
    part = ring_sum(parts[0], parts[1:], 1).astype(BF)
    part, mixed, grad_tokens = tie(part, mixed, grad_tokens)
    extra = part[4 * 96 :]
    parts = [jnp.concatenate([part[p * 96 : p * 96 + 96], extra], 0) for p in range(4)]
    part = ring_sum(parts[0], parts[1:], 0)
    mixed_out = both_rows(mixed, zl)
    grad_tokens = both_rows(grad_tokens, zl).astype(F32)
    rows, extra = part[:96].reshape(2, 48, ATT), part[96:].astype(BF)
    got = hop(jnp.concatenate([pick(rows, 1 - zh).astype(BF), extra], 0), "zh").astype(F32)
    got, mixed_out, grad_tokens, d_ffn = tie(got, mixed_out, grad_tokens, d_ffn)
    d_ffn = trade(d_ffn.reshape(2, 2, 24, 3 * SLICE), spot).astype(F32)
    rows = (pick(rows, zh) + got[:48]).reshape(2, 24, ATT)
    extra = (extra.astype(F32) + got[48:]).astype(BF)
    got = hop(jnp.concatenate([pick(rows, 1 - c).astype(BF), extra], 0), "c").astype(F32)
    sums = (extra.astype(F32) + got[24:]) * 0.5
    d_attn = pair(pick(rows, c), got[:24], c, 0)
    d_query, d_key = d_attn[0, :, :q_cols], d_attn[0, :, q_cols:]
    d_value, d_outproj = d_attn[1, :, :HD], d_attn[1, :, HD:]
    gains = sums[:4, :q_cols].astype(BF)
    gains = (gains.astype(F32) + hop(gains, "zl").astype(F32)).reshape(2, d)
    d_ffn = d_ffn.reshape(4, 24, 3, SLICE).transpose(2, 1, 0, 3).reshape(3, 24, 4 * SLICE)
    d_gate, d_up, d_down = (d_ffn[i, :, :hidden_units] for i in range(3))
    return (
        mixed_out,
        grad_tokens,
        gains[0],
        d_query,
        sums[4, :q_cols],
        d_key,
        sums[5, :HD],
        d_value,
        sums[5, HD : 2 * HD],
        d_outproj.T,
        gains[1],
        d_gate,
        d_up,
        d_down.T,
    )


def solution(mesh):
    split = Mesh(mesh.devices.reshape(4, 4, 2, 2, 2), EVERY)
    return jax.shard_map(
        on_device,
        mesh=split,
        in_specs=(
            P(WIDE, None),
            P(WIDE, None),
            P(),
            P(WIDE, "zl"),
            P("zl"),
            P(WIDE, "zl"),
            P("zl"),
            P(WIDE, "zl"),
            P("zl"),
            P("zl", WIDE),
            P(),
            P(WIDE, "zl"),
            P(WIDE, "zl"),
            P("zl", WIDE),
            P(WIDE, None),
        ),
        out_specs=(
            P(WIDE, None),
            P(WIDE, None),
            P(),
            P(WIDE, "zl"),
            P("zl"),
            P(WIDE, "zl"),
            P("zl"),
            P(WIDE, "zl"),
            P("zl"),
            P("zl", WIDE),
            P(),
            P(WIDE, "zl"),
            P(WIDE, "zl"),
            P("zl", WIDE),
        ),
        check_vma=False,
    )
```

```python
import functools

import jax
import jax.numpy as jnp
from jax import lax
from jax.experimental import pallas as pl
from jax.experimental.pallas import tpu as pltpu
from jax.sharding import Mesh, PartitionSpec as P

HD = 128
BF = jnp.bfloat16
F32 = jnp.float32
rope_base = 10000.0
norm_eps = 1e-06
WIDE = ("y", "x", "zh", "c")
EVERY = ("y", "x", "zh", "c", "zl")
SLICE = 1152
ATT = 896
HEADS = 6
STEPS = (0, 1, 3, 2)
BACK = (0, 2, 1, 3)
VEC = 16


def mm(left, right):
    return jnp.dot(left, right, preferred_element_type=F32)


def contract_rows(left, right):
    return lax.dot_general(left, right, (((0,), (0,)), ((), ())), preferred_element_type=F32)


def contract_cols(left, right):
    return lax.dot_general(left, right, (((1,), (1,)), ((), ())), preferred_element_type=F32)


def hop(value, axis, step=1):
    size = lax.axis_size(axis)
    return lax.ppermute(value, axis, [(i, (i + step) % size) for i in range(size)])


def zhop(value, step):
    return lax.ppermute(value, ("zh", "zl"), [(i, (i + step) % 4) for i in range(4)])


def plane_hop(value, step, turned):
    pairs = []
    for y in range(4):
        for x in range(4):
            for c in range(2):
                if c == turned:
                    to = (y, (x + step) % 4)
                else:
                    to = ((y + step) % 4, x)
                pairs.append(((y * 4 + x) * 2 + c, (to[0] * 4 + to[1]) * 2 + c))
    return lax.ppermute(value, ("y", "x", "c"), pairs)


def pair(mine, theirs, side, dim):
    first = jnp.where(side == 0, mine, theirs)
    second = jnp.where(side == 0, theirs, mine)
    return jnp.stack([first, second], dim)


def tie(*values):
    return lax.optimization_barrier(values)


def pick(value, index, dim=0):
    return lax.dynamic_index_in_dim(value, index, dim, keepdims=False)


def first_hops(attn, ffn, spot):
    zh, c = spot[2], spot[3]
    ffn = trade(ffn, spot).reshape(96, 3 * SLICE)
    attn = pair(pick(attn, c), hop(pick(attn, 1 - c), "c"), c, 0).reshape(48, ATT)
    return pair(attn, hop(attn, "zh"), zh, 0).reshape(96, ATT), ffn


def gather_attn(block):
    block = jnp.stack([block] + [plane_hop(block, k, 0) for k in STEPS[1:]], 0)
    pieces = [block] + [plane_hop(block, k, 1) for k in STEPS[1:]]
    return pieces, [hop(piece, "c") for piece in pieces]


def ring_sum(own, sent, turned):
    got = [plane_hop(value, k, turned).astype(F32) for k, value in zip(STEPS[1:], sent)]
    return (own.astype(F32) + got[2]) + (got[0] + got[1])


def traded(blocks, spot):
    me = spot[2] * 2 + spot[3]
    blocks = blocks.reshape((4,) + blocks.shape[2:])
    got = [pick(blocks, me)]
    for flip in (1, 2, 3):
        pairs = [(i, i ^ flip) for i in range(4)]
        got.append(lax.ppermute(pick(blocks, me ^ flip), ("zh", "c"), pairs))
    return got


def trade(blocks, spot):
    got = traded(blocks, spot)
    low = pair(got[0], got[1], spot[3], 0)
    return pair(low, pair(got[2], got[3], spot[3], 0), spot[2], 0)


def gather_tokens(value):
    pieces = [value] + [zhop(value, k) for k in STEPS[1:]]
    return pieces, [hop(piece, "c") for piece in pieces]


def send_pieces(pieces):
    return [pieces[0]] + [zhop(value, -k % 4) for k, value in zip(STEPS[1:], pieces[1:])]


def sum_pieces(pieces):
    back, ahead, far = (piece.astype(F32) for piece in pieces[1:])
    return pieces[0].astype(F32) + far + (back + ahead)


def both_rows(mine, zl):
    return pair(mine, hop(mine, "zl"), zl, 0).reshape(2 * mine.shape[0], mine.shape[1])


def own_rows(value, side):
    half = value.shape[0] // 2
    return lax.dynamic_slice_in_dim(value, side * half, half, 0)


HBM = pl.BlockSpec(memory_space=pltpu.HBM)
VMEM = pl.BlockSpec(memory_space=pltpu.VMEM)
SMEM = pl.BlockSpec(memory_space=pltpu.SMEM)


def params(mib):
    return pltpu.CompilerParams(vmem_limit_bytes=mib * 2**20)


def cost(flops, moved, exps=0):
    return pl.CostEstimate(flops=flops, bytes_accessed=moved, transcendentals=exps)


def block_rows(spot, core, outer, inner):
    y, x = spot[0], spot[1]
    far, near = STEPS[outer], STEPS[inner]
    row = jnp.where(core == 0, (y - far) & 3, (y - near) & 3)
    col = jnp.where(core == 0, (x - near) & 3, (x - far) & 3)
    return pl.multiple_of((row * 4 + col) * 96, 96)


def load_weights(spot, pieces, w):
    for side in range(2):
        core = spot[3] if side == 0 else 1 - spot[3]
        for outer in range(4):
            for inner in range(4):
                row = block_rows(spot, core, outer, inner)
                w[core, pl.ds(row, 96)] = pieces[side * 4 + outer][inner]


def halves(side, value, mine_ref, theirs_ref):
    half = value.shape[0] // 2
    low, high = value[:half], value[half:]
    first = side == 0
    mine_ref[...] = jnp.where(first, low, high)
    theirs_ref[...] = jnp.where(first, high, low).astype(BF)


def turn(value, cosine, sine):
    return value * cosine + pltpu.roll(value, HD // 2, 1) * sine


def attention_kernel(spot, h, bias, cosine, sine, keep, *rest):
    pieces = rest[:8]
    mine, theirs, attended, qkv_out, probs_out, w = rest[8:]
    scale = HD ** (-0.5)
    load_weights(spot, pieces, w)
    cos, sin = cosine[...], sine[...]
    allowed = keep[...] > 0.5
    q_cols = HEADS * HD
    first = mm(h[...], w[0]) + bias[:, :ATT]
    keys = turn(first[:, q_cols:], cos, sin).astype(BF)
    values = (mm(h[...], w[1, :, :HD]) + bias[:, ATT:]).astype(BF)
    qkv_out[:, q_cols : q_cols + HD] = keys
    qkv_out[:, q_cols + HD :] = values
    for g in range(HEADS):
        cols = slice(g * HD, (g + 1) * HD)
        query = turn(first[:, cols], cos, sin).astype(BF)
        qkv_out[:, cols] = query
        logits = jnp.where(allowed, contract_cols(query, keys) * scale, -1000000000.0)
        expo = jnp.exp(logits - jnp.max(logits, axis=-1, keepdims=True))
        probs = expo / jnp.sum(expo, axis=-1, keepdims=True)
        probs_out[g] = probs
        attended[:, cols] = mm(probs.astype(BF), values).astype(BF)
    halves(spot[4], contract_cols(attended[...], w[1, :, HD:]), mine, theirs)


def attention_forward(spot, h, bias, cosine, sine, keep, pieces):
    rows, d = h.shape
    return pl.pallas_call(
        attention_kernel,
        in_specs=[SMEM] + [VMEM] * 13,
        out_shape=(
            jax.ShapeDtypeStruct((rows // 2, d), F32),
            jax.ShapeDtypeStruct((rows // 2, d), BF),
            jax.ShapeDtypeStruct((rows, HEADS * HD), BF),
            jax.ShapeDtypeStruct((rows, (HEADS + 2) * HD), BF),
            jax.ShapeDtypeStruct((HEADS, rows, rows), F32),
        ),
        scratch_shapes=[pltpu.VMEM((2, d, ATT), BF)],
        compiler_params=params(24),
        cost_estimate=cost(2_200_000_000, 12_000_000, 400_000),
        name="attention",
    )(spot, h, bias, cosine, sine, keep, *pieces)


def attention_back_kernel(
    spot, mine_in, theirs_in, h, tokens, factor, gain_two, attended, qkv, probs, cosine, sine, *rest
):
    pieces = rest[:8]
    mine, theirs, grads_mine, grads_theirs = rest[8:12]
    w, branch, grad_qkv, grads = rest[12:]
    scale = HD ** (-0.5)
    load_weights(spot, pieces, w)
    half, d = mine_in.shape
    zl = spot[4]
    branch[pl.ds(pl.multiple_of(zl * half, half), half)] = mine_in[...]
    branch[pl.ds(pl.multiple_of((1 - zl) * half, half), half)] = theirs_in[...]
    cos, sin = cosine[...], -sine[...]
    q_cols = HEADS * HD
    keys = qkv[:, q_cols : q_cols + HD]
    values = qkv[:, q_cols + HD :]
    grad_att = mm(branch[...], w[1, :, HD:]).astype(BF)
    grad_key = jnp.zeros((2 * half, HD), F32)
    grad_value = jnp.zeros((2 * half, HD), F32)
    for g in range(HEADS):
        cols = slice(g * HD, (g + 1) * HD)
        grad_head = grad_att[:, cols]
        grad_probs = contract_cols(grad_head, values)
        prob = probs[g]
        inner = jnp.sum(prob * grad_probs, axis=-1, keepdims=True)
        grad_logits = (prob * (grad_probs - inner)).astype(BF)
        grad_query = mm(grad_logits, keys) * scale
        grad_qkv[:, cols] = turn(grad_query, cos, sin).astype(BF)
        grad_key += contract_rows(grad_logits, qkv[:, cols])
        grad_value += contract_rows(prob.astype(BF), grad_head)
    grad_qkv[:, q_cols : q_cols + HD] = turn(grad_key * scale, cos, sin).astype(BF)
    grad_qkv[:, q_cols + HD :] = grad_value.astype(BF)
    grads[0] = contract_rows(h[...], grad_qkv[:, :ATT]).astype(BF)
    grads[1, :, :HD] = contract_rows(h[...], grad_qkv[:, ATT:]).astype(BF)
    grads[1, :, HD:] = contract_rows(branch[...], attended[...]).astype(BF)
    grad_h = contract_cols(grad_qkv[:, :ATT], w[0])
    grad_h += contract_cols(grad_qkv[:, ATT:], w[1, :, :HD])
    halves(zl, grad_h, mine, theirs)
    bias = jnp.sum(grad_qkv[...].astype(F32), axis=0, keepdims=True)
    gain_one = jnp.sum(grad_h * (tokens[...].astype(F32) * factor[...]), axis=0, keepdims=True)
    spare = jnp.zeros((1, ATT - q_cols), F32)
    lines = [gain_one[:, :q_cols], gain_one[:, q_cols:]]
    lines += [gain_two[:, :q_cols], gain_two[:, q_cols:], bias[:, :q_cols]]
    lines = [jnp.concatenate([line, spare], 1) for line in lines]
    lines.append(jnp.concatenate([bias[:, q_cols:], jnp.zeros((1, ATT - 2 * HD), F32)], 1))
    lines.append(jnp.zeros((VEC - 6, ATT), F32))
    vectors = jnp.concatenate(lines, 0).astype(BF)
    for side, out in enumerate((grads_mine, grads_theirs)):
        core = spot[3] if side == 0 else 1 - spot[3]
        for outer in range(4):
            for inner in range(4):
                row = block_rows(spot, core, BACK[outer], BACK[inner])
                out[outer, inner * 96 : inner * 96 + 96] = grads[core, pl.ds(row, 96)]
            out[outer, 4 * 96 :] = vectors


def attention_backward(
    spot, mine, theirs, h, tokens, factor, gain_two, attended, qkv, probs, cosine, sine, pieces
):
    rows, d = h.shape
    blocks = jax.ShapeDtypeStruct((4, 4 * 96 + VEC, ATT), BF)
    return pl.pallas_call(
        attention_back_kernel,
        in_specs=[SMEM] + [VMEM] * 19,
        out_shape=(
            jax.ShapeDtypeStruct((rows // 2, d), F32),
            jax.ShapeDtypeStruct((rows // 2, d), BF),
            blocks,
            blocks,
        ),
        scratch_shapes=[
            pltpu.VMEM((2, d, ATT), BF),
            pltpu.VMEM((rows, d), BF),
            pltpu.VMEM((rows, (HEADS + 2) * HD), BF),
            pltpu.VMEM((2, d, ATT), BF),
        ],
        compiler_params=params(32),
        cost_estimate=cost(4_300_000_000, 20_000_000),
        name="attention_back",
    )(spot, mine, theirs, h, tokens, factor, gain_two, attended, qkv, probs, cosine, sine, *pieces)


CHUNKS = [(start, min(256, SLICE - start)) for start in range(0, SLICE, 256)]


def block_places(zl):
    return zl, 3 * (1 - zl), 1 + zl, 2 + zl


def hidden_kernel(spot, h0, h1, h2, h3, g, w, h, act, sems):
    rows = h0.shape[0]
    copies = []
    for i, (place, piece) in enumerate(zip(block_places(spot[4]), (h0, h1, h2, h3))):
        target = h.at[pl.ds(pl.multiple_of(place * rows, rows), rows)]
        copies.append(pltpu.make_async_copy(piece, target, sems.at[i]))
    for copy in copies:
        copy.start()
    for copy in copies:
        copy.wait()
    for start, size in CHUNKS:
        cols = [slice(part * SLICE + start, part * SLICE + start + size) for part in range(3)]
        gate = mm(h[...], w[:, cols[0]])
        up_act = mm(h[...], w[:, cols[1]])
        grad = mm(g[...], w[:, cols[2]])
        sigma = jax.nn.sigmoid(gate)
        swish = gate * sigma
        act[:, cols[0]] = (grad * up_act * sigma * (1.0 + gate * (1.0 - sigma))).astype(BF)
        act[:, cols[1]] = (grad * swish).astype(BF)
        act[:, cols[2]] = (swish * up_act).astype(BF)


def hidden_act(spot, pieces, g, w):
    rows, d = g.shape
    return pl.pallas_call(
        hidden_kernel,
        in_specs=[SMEM] + [HBM] * 4 + [VMEM] * 2,
        out_specs=(VMEM, VMEM),
        out_shape=(
            jax.ShapeDtypeStruct((rows, d), BF),
            jax.ShapeDtypeStruct((rows, 3 * SLICE), BF),
        ),
        scratch_shapes=[pltpu.SemaphoreType.DMA((4,))],
        compiler_params=params(24),
        cost_estimate=cost(5_400_000_000, 20_000_000, 600_000),
        name="hidden",
    )(spot, *pieces, g, w)


def back_kernel(start, stop, act, w, out):
    for row in range(0, w.shape[0], 256):
        cols = slice(row, row + 256)
        out[:, cols] = contract_cols(act[:, start:stop], w[cols, : stop - start]).astype(BF)


def back_sum_kernel(start, stop, spot, act, w, other, out0, out1, out2, out3, part):
    rows = out0.shape[0]
    for row in range(0, w.shape[0], 256):
        cols = slice(row, row + 256)
        part[...] = contract_cols(act[:, start:stop], w[cols, : stop - start])
        part[...] += other[:, cols].astype(F32)
        for place, out in zip(block_places(spot[4]), (out0, out1, out2, out3)):
            block = pl.ds(pl.multiple_of(place * rows, rows), rows)
            out[:, cols] = part[block].astype(out.dtype)


def times_weights(start, stop, act, w, spot=None, other=None):
    rows, d = act.shape[0], w.shape[0]
    if other is None:
        shapes = pltpu.HBM((rows, d), BF)
        kernel, args, scratch = back_kernel, (act, w), []
    else:
        shapes = tuple(pltpu.HBM((rows // 4, d), F32 if i == 0 else BF) for i in range(4))
        kernel, args = back_sum_kernel, (spot, act, w, other)
        scratch = [pltpu.VMEM((rows, 256), F32)]
    return pl.pallas_call(
        functools.partial(kernel, start, stop),
        in_specs=[SMEM] * (len(args) - 2 - (other is not None)) + [VMEM] * (2 + (other is not None)),
        out_specs=jax.tree.map(lambda _: VMEM, shapes),
        out_shape=shapes,
        scratch_shapes=scratch,
        compiler_params=params(18),
        cost_estimate=cost(2 * rows * d * (stop - start), 10_000_000),
        name="hidden_back",
    )(*args)


def grad_hidden_input(act, w, *more):
    return times_weights(0, 2 * SLICE, act, w, *more)


def mixed_part(act, w, *more):
    return times_weights(2 * SLICE, 3 * SLICE, act, w, *more)


TILE = 256


def weights_kernel(h_mine, h_theirs, g_mine, g_theirs, act_mine, act_theirs, out, buf, sems):
    tiles = out.shape[0] // TILE

    def copy(at):
        row = pl.multiple_of(at * TILE, TILE)
        return pltpu.make_async_copy(buf.at[at & 1], out.at[pl.ds(row, TILE)], sems.at[at & 1])

    def body(step, _):
        @pl.when(step >= 2)
        def _():
            copy(step - 2).wait()

        rows = pl.ds(pl.multiple_of(step * TILE, TILE), TILE)
        for left, start, stop in ((0, 0, 2 * SLICE), (1, 2 * SLICE, 3 * SLICE)):
            mine, theirs = ((h_mine, h_theirs), (g_mine, g_theirs))[left]
            part = contract_rows(mine[:, rows], act_mine[:, start:stop])
            part += contract_rows(theirs[:, rows], act_theirs[:, start:stop])
            buf[step & 1, :, start:stop] = part.astype(BF)
        copy(step).start()
        return 0

    lax.fori_loop(0, tiles, body, 0)
    copy(tiles - 2).wait()
    copy(tiles - 1).wait()


def hidden_weights(h_mine, h_theirs, g_mine, g_theirs, act_mine, act_theirs):
    rows, d = h_mine.shape
    return pl.pallas_call(
        weights_kernel,
        in_specs=[VMEM] * 6,
        out_specs=HBM,
        out_shape=pltpu.HBM((d, 3 * SLICE), BF),
        scratch_shapes=[
            pltpu.VMEM((2, TILE, 3 * SLICE), BF),
            pltpu.SemaphoreType.DMA((2,)),
        ],
        compiler_params=params(18),
        cost_estimate=cost(10_900_000_000, 24_000_000),
        name="hidden_weights",
    )(h_mine, h_theirs, g_mine, g_theirs, act_mine, act_theirs)


def place_kernel(spot, b0, b1, b2, b3, gate, up, down, whole):
    me = spot[2] * 2 + spot[3]
    for flip, block in enumerate((b0, b1, b2, b3)):
        start = pl.multiple_of((me ^ flip) * SLICE, 128)
        for part in range(3):
            cols = slice(part * SLICE, (part + 1) * SLICE)
            whole[part, :, pl.ds(start, SLICE)] = block[:, cols].astype(F32)
    for part, out in enumerate((gate, up, down)):
        out[...] = whole[part, :, : out.shape[1]]


def place_blocks(spot, blocks, units):
    rows = blocks[0].shape[0]
    return pl.pallas_call(
        place_kernel,
        in_specs=[SMEM] + [VMEM] * 4,
        out_shape=[jax.ShapeDtypeStruct((rows, units), F32)] * 3,
        scratch_shapes=[pltpu.VMEM((3, rows, 4 * SLICE), F32)],
        compiler_params=params(12),
        cost_estimate=cost(0, 2_000_000),
        name="place",
    )(spot, *blocks)


def doc_layout(lengths, count):
    ends = jnp.cumsum(lengths)
    starts = ends - lengths
    place = jnp.arange(count, dtype=jnp.int32)
    segment = jnp.sum((place[:, None] >= ends[None, :]).astype(jnp.int32), axis=1)
    labels = jnp.arange(lengths.shape[0], dtype=jnp.int32)
    first = jnp.sum(jnp.where(segment[:, None] == labels[None, :], starts[None, :], 0), axis=1)
    return (segment, place - first, place)


def on_device(
    tokens,
    doc_lengths,
    norm_gain1,
    w_query,
    b_query,
    w_key,
    b_key,
    w_value,
    b_value,
    w_out,
    norm_gain2,
    w_gate,
    w_up,
    w_down,
    out_grad,
):
    spot = tuple(lax.axis_index(axis) for axis in EVERY)
    y, x, zh, c, zl = spot
    place_of = jnp.stack(spot)
    rows, d = tokens.shape
    hidden_units = w_gate.shape[1]
    pad = 4 * SLICE - hidden_units
    q_cols = HEADS * HD

    attn = jnp.concatenate([w_query, w_key, w_value, w_out.T], 1)
    attn = jnp.stack([attn[:, :ATT], attn[:, ATT:]], 0)
    ffn = jnp.stack([w_gate, w_up, w_down.T], 1)
    ffn = jnp.pad(ffn, ((0, 0), (0, 0), (0, pad))).reshape(24, 3, 4, SLICE)
    ffn = ffn.transpose(2, 0, 1, 3).reshape(2, 2, 24, 3 * SLICE)
    segment, position, place = doc_layout(doc_lengths[0], rows)
    inverse = rope_base ** (-jnp.arange(0, HD, 2, dtype=F32) / HD)
    angle = position.astype(F32)[:, None] * inverse[None, :]
    cosine, sine = jnp.cos(angle), jnp.sin(angle)
    cosine = jnp.concatenate([cosine, cosine], 1)
    sine = jnp.concatenate([-sine, sine], 1)
    keep = (segment[:, None] == segment[None, :]) & (place[None, :] <= place[:, None])
    inputs = tokens.astype(F32)
    factor_one = lax.rsqrt(jnp.mean(inputs * inputs, axis=-1, keepdims=True) + norm_eps)
    normed_one = inputs * factor_one
    h_one = (normed_one * norm_gain1).astype(BF)
    bias = jnp.concatenate([b_query, b_key, b_value])[None]
    attn, ffn = first_hops(attn, ffn, spot)
    ffn_full = lax.all_gather(ffn, ("y", "x"), axis=0, tiled=True)
    attn, h_one, cosine, sine, keep = tie(attn, h_one, cosine, sine, keep.astype(F32))
    far = hop(out_grad, "zh")
    near_theirs, far_theirs = hop(out_grad, "c"), hop(far, "c")
    mine, theirs = gather_attn(attn)
    pieces, far, near_theirs, far_theirs = tie(mine + theirs, far, near_theirs, far_theirs)

    mine, theirs, attended, qkv, probs = attention_forward(
        place_of, h_one, bias, cosine, sine, keep, pieces
    )
    theirs, far, near_theirs, far_theirs = tie(theirs, far, near_theirs, far_theirs)
    grad_mine = jnp.concatenate([out_grad, far], 0)
    grad_theirs = jnp.concatenate([near_theirs, far_theirs], 0)
    theirs, grad_mine, grad_theirs = tie(hop(theirs, "zl"), grad_mine, grad_theirs)
    resid = own_rows(tokens, zl).astype(F32) + mine + theirs.astype(F32)

    factor_two = lax.rsqrt(jnp.mean(resid * resid, axis=-1, keepdims=True) + norm_eps)
    normed_two = resid * factor_two
    h_two = (normed_two * norm_gain2).astype(BF)
    mine = [h_two] + [zhop(h_two, k) for k in STEPS[1:]]
    mine[1], ffn_full = tie(mine[1], ffn_full)
    theirs = [hop(piece, "c") for piece in mine]
    h_mine, act_mine = hidden_act(place_of, mine, grad_mine, ffn_full)
    h_theirs, act_theirs = hidden_act(place_of, theirs, grad_theirs, ffn_full)
    back = hop(grad_hidden_input(act_theirs, ffn_full), "c")
    back = grad_hidden_input(act_mine, ffn_full, place_of, back)
    back, act_mine, act_theirs = tie(back, act_mine, act_theirs)
    d_ffn = hidden_weights(h_mine, h_theirs, grad_mine, grad_theirs, act_mine, act_theirs)
    d_ffn, back, act_mine, act_theirs = tie(d_ffn, send_pieces(back), act_mine, act_theirs)
    grad_h_two = sum_pieces(back)
    d_ffn = lax.psum_scatter(d_ffn, ("y", "x"), scatter_dimension=0, tiled=True)

    gain_two = jnp.sum(grad_h_two * normed_two, axis=0, keepdims=True)
    grad_n_two = grad_h_two * norm_gain2
    grad_resid = own_rows(out_grad, zl).astype(F32) + factor_two * (
        grad_n_two - normed_two * jnp.mean(grad_n_two * normed_two, axis=-1, keepdims=True)
    )
    grad_branch, act_mine, act_theirs = tie(grad_resid.astype(BF), act_mine, act_theirs)
    down_full = ffn_full[:, 2 * SLICE :]
    mixed = hop(mixed_part(act_theirs, down_full), "c")
    mixed = mixed_part(act_mine, down_full, place_of, mixed)
    branch_theirs, mixed = tie(hop(grad_branch, "zl"), mixed)
    mixed = (resid + sum_pieces(send_pieces(mixed))).astype(BF)

    mine, theirs, grads_mine, grads_theirs = attention_backward(
        place_of,
        grad_branch,
        branch_theirs,
        h_one,
        tokens,
        factor_one,
        gain_two,
        attended,
        qkv,
        probs,
        cosine,
        sine,
        pieces,
    )
    grads_theirs = hop(grads_theirs, "c")
    grad_h_one = mine + hop(theirs, "zl").astype(F32)
    my_normed = own_rows(normed_one, zl)
    grad_n_one = grad_h_one * norm_gain1
    grad_tokens = grad_resid + own_rows(factor_one, zl) * (
        grad_n_one - my_normed * jnp.mean(grad_n_one * my_normed, axis=-1, keepdims=True)
    )
    grad_tokens = grad_tokens.astype(BF)

    parts = [(grads_mine[p].astype(F32) + grads_theirs[p].astype(F32)).astype(BF) for p in range(4)]
    part = ring_sum(parts[0], parts[1:], 1).astype(BF)
    part, mixed, grad_tokens = tie(part, mixed, grad_tokens)
    extra = part[4 * 96 :]
    parts = [jnp.concatenate([part[p * 96 : p * 96 + 96], extra], 0) for p in range(4)]
    part = ring_sum(parts[0], parts[1:], 0)
    mixed_out = both_rows(mixed, zl)
    grad_tokens = both_rows(grad_tokens, zl).astype(F32)
    rows, extra = part[:96].reshape(2, 48, ATT), part[96:].astype(BF)
    got = hop(jnp.concatenate([pick(rows, 1 - zh).astype(BF), extra], 0), "zh").astype(F32)
    got, mixed_out, grad_tokens, d_ffn = tie(got, mixed_out, grad_tokens, d_ffn)
    d_ffn = traded(d_ffn.reshape(2, 2, 24, 3 * SLICE), spot)
    d_gate, d_up, d_down = place_blocks(place_of, d_ffn, hidden_units)
    rows = (pick(rows, zh) + got[:48]).reshape(2, 24, ATT)
    extra = (extra.astype(F32) + got[48:]).astype(BF)
    got = hop(jnp.concatenate([pick(rows, 1 - c).astype(BF), extra], 0), "c").astype(F32)
    sums = (extra.astype(F32) + got[24:]) * 0.5
    d_attn = pair(pick(rows, c), got[:24], c, 0)
    d_query, d_key = d_attn[0, :, :q_cols], d_attn[0, :, q_cols:]
    d_value, d_outproj = d_attn[1, :, :HD], d_attn[1, :, HD:]
    gains = sums[:4, :q_cols].astype(BF)
    gains = (gains.astype(F32) + hop(gains, "zl").astype(F32)).reshape(2, d)
    return (
        mixed_out,
        grad_tokens,
        gains[0],
        d_query,
        sums[4, :q_cols],
        d_key,
        sums[5, :HD],
        d_value,
        sums[5, HD : 2 * HD],
        d_outproj.T,
        gains[1],
        d_gate,
        d_up,
        d_down.T,
    )


def solution(mesh):
    split = Mesh(mesh.devices.reshape(4, 4, 2, 2, 2), EVERY)
    return jax.shard_map(
        on_device,
        mesh=split,
        in_specs=(
            P(WIDE, None),
            P(WIDE, None),
            P(),
            P(WIDE, "zl"),
            P("zl"),
            P(WIDE, "zl"),
            P("zl"),
            P(WIDE, "zl"),
            P("zl"),
            P("zl", WIDE),
            P(),
            P(WIDE, "zl"),
            P(WIDE, "zl"),
            P("zl", WIDE),
            P(WIDE, None),
        ),
        out_specs=(
            P(WIDE, None),
            P(WIDE, None),
            P(),
            P(WIDE, "zl"),
            P("zl"),
            P(WIDE, "zl"),
            P("zl"),
            P(WIDE, "zl"),
            P("zl"),
            P("zl", WIDE),
            P(),
            P(WIDE, "zl"),
            P(WIDE, "zl"),
            P("zl", WIDE),
        ),
        check_vma=False,
    )
```
